32 devices in a mesh: grp: 4 (over y, x), ep: 8 (over z, core).
Axes of the slice: x: 2, y: 2, z: 4, core: 2. Of those that a mesh axis runs over, the one named last changes fastest.
Arguments:
- tokens: bfloat16 [256, 4096], P(('grp', 'ep')), may hold values from -6 to 6
- expert_ids: int32 [256, 8], P(('grp', 'ep')), may hold values from 0 to 15, all different within a row; in each aligned block of 8 rows (0 to 7, 8 to 15, ...) at most 8 rows name the same one
- gate_weights: float32 [256, 8], P(('grp', 'ep')), may hold values from 0.1 to 1
- w_gate: bfloat16 [8, 4096, 2048], P('ep', None, 'grp'), may hold values from -0.09375 to 0.09375
- w_up: bfloat16 [8, 4096, 2048], P('ep', None, 'grp'), may hold values from -0.09375 to 0.09375
- w_down: bfloat16 [8, 1024, 8192], P('ep', None, 'grp'), may hold values from -0.1875 to 0.1875
- norm_gain: float32 [4096], replicated, may hold values from 0.1 to 1.9
Outputs:
- scored: bfloat16 [256, 4096], P(('grp', 'ep'))
The draws below stay inside these ranges and needn't reach their ends.
Inputs may be any that keep to these rules, and one draw needn't show every extreme that they name: `expert_ids`: each row names 8 different experts. Among the 8 rows of one device no expert is named by more than 8 rows, and in some devices' rows an expert is named by exactly 8.
All inputs are finite; a program needn't handle non-finite values.
Results may differ from the reference program's by a relative error of at most 0.0043.
Values may be sent and summed in bfloat16 or wider, within the bound.
A program may use at most 64 MiB of HBM per device.

```python
import math
import jax
import jax.numpy as jnp
import numpy as np
from jax import lax

D = 4096
TOP = 8
FF = 1024
TOK_DEV = 8
EXPERTS = 16
CAP = 8
TOKENS = 256
N_GRP = 4
N_EP = 8


def levels(stream_key, extent, pieces, low, largest):
    gain = 1.0
    for axis_at, blocks in pieces:
        steps = jax.random.uniform(jax.random.fold_in(jax.random.fold_in(stream_key, 6), axis_at), (blocks,), jnp.float32, low / len(pieces), largest / len(pieces))
        gain = gain * jnp.repeat(jnp.exp(steps), extent[axis_at] // blocks).reshape((-1,) + (1,) * (len(extent) - 1 - axis_at))
    return gain


def assign_block(stream_key, own, number, rows, number_of, top, bound, slope):
    order = jax.random.permutation(stream_key, number_of)
    heavy_load, usual = shares(number_of, rows * top, bound, slope, True), shares(number_of, rows * top, bound, slope, False)
    places = jnp.arange(number_of)

    def named(sizes, turn):
        used = int((sizes > 0).sum())
        fixed = max(1, used // 4)
        moved = fixed + (places - fixed + turn * (used - fixed)) % max(1, number_of - fixed)
        return jnp.zeros((number_of,), jnp.int32).at[order[jnp.where(places < fixed, places, moved)]].set(jnp.asarray(sizes, jnp.int32))

    sizes = jnp.where(number % 4 == 0, named(heavy_load, number // 4), named(usual, number - number // 4 - 1))
    mixed = jax.random.permutation(jax.random.fold_in(own, 3), number_of)
    source_of, receiver = mixed[0:number_of // 2 * 2:2], mixed[1:number_of // 2 * 2:2]
    margin = jnp.minimum(sizes[source_of] - 1, bound - sizes[receiver]) // 2
    margin = jnp.where((source_of == order[0]) | (receiver == order[0]) | (sizes[receiver] == 0), 0, jnp.maximum(margin, 0))
    moved = jax.random.randint(jax.random.fold_in(own, 4), (number_of // 2,), 0, 1 << 20) % (margin + 1)
    sizes = sizes.at[source_of].add(-moved).at[receiver].add(moved)
    members = jnp.searchsorted(jnp.cumsum(sizes), jnp.arange(rows * top), side="right").astype(jnp.int32)
    grid = members.reshape(top, rows).T
    grid = grid[jax.random.permutation(jax.random.fold_in(own, 1), rows)]
    turn = jax.random.randint(jax.random.fold_in(own, 2), (rows, 1), 0, top)
    return jnp.take_along_axis(grid, (jnp.arange(top)[None, :] + turn) % top, axis=1)


def shares(count, total, most, slope, full):
    weights = [(1 << 20) // math.isqrt(rank ** slope) + 1 for rank in range(1, count + 1)]
    largest = most if full else min(most, max(-(-total // count), total * weights[0] // sum(weights)))
    least = 1 if total - largest >= count - 1 else 0
    counts, surplus = [largest] + [least] * (count - 1), total - largest - least * (count - 1)
    while surplus > 0:
        free = [i for i in range(1, count) if counts[i] < largest] or [i for i in range(1, count) if counts[i] < most]
        mass, left = sum([weights[i] for i in free]), surplus
        for i in free:
            extra = min(most - counts[i], max(1, left * weights[i] // mass), surplus)
            counts[i] = counts[i] + extra
            surplus = surplus - extra
    return np.array(counts)


def normal_values(rng, dims, scale, reach, split=(), held_as=jnp.bfloat16):
    result = jax.random.normal(rng, dims, jnp.float32) * scale
    if len(split) > 0:
        result = levels(rng, dims, split, -0.22, 0.18) * result
    return jnp.clip(result, min=-reach, max=reach).astype(held_as)


def setup_inputs(seed: int = 0) -> dict:
    arg_keys = jax.random.split(jax.random.key(seed), 8)
    tokens = normal_values(arg_keys[0], (TOKENS, D), 1.0, 6.0, ((0, 32),))
    expert_ids_keys = jax.random.split(jax.random.fold_in(arg_keys[1], 1), TOKENS // TOK_DEV)
    expert_ids_turns = jax.random.permutation(jax.random.fold_in(arg_keys[1], 3), TOKENS // TOK_DEV)
    expert_ids = jax.vmap(lambda own, number: assign_block(jax.random.fold_in(arg_keys[1], 2), own, number, TOK_DEV, EXPERTS, TOP, CAP, 2))(expert_ids_keys, expert_ids_turns).reshape((TOKENS, TOP))
    gate_weights = jnp.clip(jnp.exp(math.log(1.0) - 2.3025851 * jax.random.uniform(arg_keys[2], (TOKENS, TOP), jnp.float32) ** levels(arg_keys[2], (TOKENS, TOP), ((0, 32),), -0.2, 0.2)), 0.1, 1.0)
    w_gate = normal_values(arg_keys[3], (N_EP, D, 2 * FF), D ** -0.5, 0.09375, ((0, 8), (2, 4)))
    w_up = normal_values(arg_keys[4], (N_EP, D, 2 * FF), D ** -0.5, 0.09375, ((0, 8), (2, 4)))
    w_down = normal_values(arg_keys[5], (N_EP, FF, 2 * D), FF ** -0.5, 0.1875, ((0, 8), (2, 4)))
    norm_gain = jnp.clip(1.0 + 0.18 * jax.random.normal(arg_keys[6], (D,), jnp.float32), 0.1, 1.9)
    return {"tokens": tokens, "expert_ids": expert_ids, "gate_weights": gate_weights, "w_gate": w_gate, "w_up": w_up, "w_down": w_down, "norm_gain": norm_gain}


def reference(tokens, expert_ids, gate_weights, w_gate, w_up, w_down, norm_gain):
    width = tokens.shape[1]
    hidden_all = w_down.shape[1]
    limit = N_GRP * N_EP * CAP
    experts = 2 * w_gate.shape[0]

    def one_expert(moe, expert):
        hits = expert_ids == expert
        weight = lax.optimization_barrier(jnp.sum(jnp.where(hits, gate_weights, jnp.float32(0.0)), axis=1))
        member = jnp.any(hits, axis=1)
        picked = jnp.nonzero(member, size=limit, fill_value=0)[0].astype(jnp.int32)
        valid = (jnp.arange(limit) < jnp.sum(member.astype(jnp.int32))).astype(jnp.float32)
        rows_in = tokens[picked]
        pair_idx = (expert // 2).astype(jnp.int32)
        half_idx = (expert % 2).astype(jnp.int32)
        gate_pair = lax.dynamic_index_in_dim(w_gate, pair_idx, 0, keepdims=False)
        up_pair = lax.dynamic_index_in_dim(w_up, pair_idx, 0, keepdims=False)
        down_pair = lax.dynamic_index_in_dim(w_down, pair_idx, 0, keepdims=False)
        gate_cols = lax.dynamic_slice_in_dim(gate_pair, half_idx * hidden_all, hidden_all, 1)
        up_cols = lax.dynamic_slice_in_dim(up_pair, half_idx * hidden_all, hidden_all, 1)
        down_cols = lax.dynamic_slice_in_dim(down_pair, half_idx * width, width, 1)
        gate_part = jnp.dot(rows_in, gate_cols, preferred_element_type=jnp.float32)
        up_part = jnp.dot(rows_in, up_cols, preferred_element_type=jnp.float32)
        hidden = (jax.nn.silu(gate_part) * up_part).astype(jnp.bfloat16)
        expert_out = jnp.dot(hidden, down_cols, preferred_element_type=jnp.float32).astype(jnp.bfloat16)
        scale_rows = weight[picked] * valid
        moe = moe.at[picked].add(expert_out.astype(jnp.float32) * scale_rows[:, None])
        return (moe, None)
    start = jnp.zeros(tokens.shape, jnp.float32)
    moe, unused = lax.scan(one_expert, start, jnp.arange(experts, dtype=jnp.int32))
    mixed = tokens.astype(jnp.float32) + moe
    factor = lax.rsqrt(lax.optimization_barrier(jnp.mean(mixed * mixed, axis=1, keepdims=True)) + 1e-06)
    return (mixed * factor * norm_gain).astype(jnp.bfloat16)
```

```python
import functools

import jax
import jax.numpy as jnp
from jax import lax
from jax.experimental import pallas as pl
from jax.experimental.pallas import tpu as pltpu
from jax.sharding import PartitionSpec as P

LANES = 128
MESH = pl.DeviceIdType.MESH


def dot32(a, b):
    return jnp.dot(a, b, preferred_element_type=jnp.float32)


def fused_kernel(
    nz, experts,
    tok_ref, ids_ref, gates_ref, gain_ref, wg_hbm, wu_hbm, wd_hbm, out_ref,
    wg, wu, wd, s_out, s_in, xm, xs, hid_out, hid_in, part_out, part_in, ret_out, ret_in, fin_out, fin_in,
    w_sem, s_sem, z_sem, x_sem, y_sem, dx_sem, dy_sem, sib_sem, hid_sem, part_sem, ret_sem, fin_sem,
):
    f32, bf16 = jnp.float32, jnp.bfloat16
    rows, width = tok_ref.shape
    half = width // 2
    quarter = width // 4
    block = 2 * rows
    column = nz * block
    ff_half = wg.shape[2]
    g, p = lax.axis_index("grp"), lax.axis_index("ep")
    y, x = g // 2, g % 2
    z, c = p // 2, p % 2
    ox, oy, oc = 1 - x, 1 - y, 1 - c

    def dev(xx, yy, zz, cc):
        return (yy * 2 + xx, zz * 2 + cc)

    def remote(src, dst, sems, idx, to):
        return pltpu.make_async_remote_copy(
            src_ref=src, dst_ref=dst, send_sem=sems.at[0, idx], recv_sem=sems.at[1, idx],
            device_id=to, device_id_type=MESH,
        )

    sibling = dev(x, y, z, oc)
    x_peer = dev(ox, y, z, c)
    y_peer = dev(x, oy, z, c)

    loads = []
    n = 0
    for mine, at_k in ((0, c), (1, oc)):
        for src, dst in ((wg_hbm, wg), (wu_hbm, wu)):
            span = pl.ds(pl.multiple_of(at_k * half, half), half)
            loads.append(pltpu.make_async_copy(src.at[0, span, :], dst.at[mine], w_sem.at[n]))
            n += 1
    for mine, at_k in ((0, x), (1, ox)):
        span = pl.ds(pl.multiple_of(at_k * ff_half, ff_half), ff_half)
        loads.append(pltpu.make_async_copy(wd_hbm.at[0, span, :], wd.at[mine], w_sem.at[n]))
        n += 1

    barrier = pltpu.get_barrier_semaphore()
    greeted = 0
    for dy in range(2):
        for dx in range(2):
            for dz in range(nz):
                if dy or dx or dz:
                    to = dev((x + dx) % 2, (y + dy) % 2, (z + dz) % nz, c)
                    pl.semaphore_signal(barrier, inc=1, device_id=to, device_id_type=MESH)
                    greeted += 1
    pl.semaphore_signal(barrier, inc=1, device_id=sibling, device_id_type=MESH)
    greeted += 1
    for load in loads:
        load.start()

    lane = lax.broadcasted_iota(jnp.int32, (rows, LANES), 1)
    table = jnp.zeros((rows, LANES), f32)
    for k in range(ids_ref.shape[1]):
        table += jnp.where(ids_ref[:, k : k + 1] == lane % experts, gates_ref[:, k : k + 1], f32(0.0))
    tok = tok_ref[...].astype(f32)
    first = c == 0
    mine_half = jnp.where(first, tok[:, :half], tok[:, half:])
    s_out[:, :half] = jnp.where(first, tok[:, half:], tok[:, :half])
    s_out[:, half:] = table
    pl.semaphore_wait(barrier, greeted)

    sends = []

    def go(copy):
        copy.start()
        sends.append(copy)
        return copy

    swap = go(remote(s_out, s_in, s_sem, 0, sibling))
    swap.wait_recv()
    theirs, their_table = s_in[:, :half], s_in[:, half:]

    def both(a, b):
        return jnp.where(first, jnp.concatenate([a, b], axis=0), jnp.concatenate([b, a], axis=0))

    pair_table = both(table, their_table)
    high = pair_table.astype(bf16)
    rest = pair_table - high.astype(f32)
    middle = rest.astype(bf16)
    low = (rest - middle.astype(f32)).astype(bf16)
    part = lax.broadcasted_iota(jnp.int32, (block, LANES), 1) // experts
    coded = jnp.where(
        part == 0, high.astype(f32),
        jnp.where(part == 1, middle.astype(f32), jnp.where(part == 2, low.astype(f32), f32(0.0))),
    )

    def spot(xx, i):
        return pl.ds(pl.multiple_of(xx * column + i * block, block), block)

    def whole(xx):
        return pl.ds(pl.multiple_of(xx * column, column), column)

    xm[0, spot(x, 0), :] = jnp.concatenate([both(mine_half, theirs), coded], axis=1).astype(bf16)

    z_copy = [None] + [
        remote(xm.at[0, spot(x, 0), :], xm.at[0, spot(x, i), :], z_sem, i, dev(x, y, (z + i) % nz, c))
        for i in range(1, nz)
    ]
    x_copy = [remote(xm.at[0, spot(x, i), :], xm.at[0, spot(x, i), :], x_sem, i, x_peer) for i in range(nz)]
    x_land = [remote(xm.at[0, spot(ox, i), :], xm.at[0, spot(ox, i), :], x_sem, i, x_peer) for i in range(nz)]
    y_copy = [remote(xm.at[0, spot(x, i), :], xm.at[1, spot(x, i), :], y_sem, i, y_peer) for i in range(nz)]
    by_y = [i for i in range(nz) if i % 4 in (1, 2)]
    d_copy, d_land = [], []
    for i in range(nz):
        if i in by_y:
            d_copy.append(remote(xm.at[0, spot(ox, i), :], xm.at[1, spot(ox, i), :], dy_sem, i, y_peer))
            d_land.append(d_copy[-1])
        else:
            d_copy.append(remote(xm.at[1, spot(x, i), :], xm.at[1, spot(x, i), :], dx_sem, i, x_peer))
            d_land.append(remote(xm.at[1, spot(ox, i), :], xm.at[1, spot(ox, i), :], dx_sem, i, x_peer))
    sib_copy = [
        [remote(xm.at[s, whole(xx), :], xs.at[s, whole(xx), :], sib_sem, 2 * s + j, sibling)
         for j, xx in enumerate((x, ox))]
        for s in range(2)
    ]

    for i in range(1, nz):
        go(z_copy[i])
    go(x_copy[0])
    go(y_copy[0])
    for i in range(1, nz):
        z_copy[i].wait_recv()
        go(x_copy[i])
        go(y_copy[i])
    go(sib_copy[0][0])
    for i in range(nz):
        x_land[i].wait_recv()
        if i in by_y:
            go(d_copy[i])
        y_copy[i].wait_recv()
        if i not in by_y:
            go(d_copy[i])
    go(sib_copy[0][1])
    go(sib_copy[1][0])

    def front(s):
        gate = dot32(xm[s, :, :half], wg[0])
        up = dot32(xm[s, :, :half], wu[0])
        if s == 0:
            for load in loads[2:4]:
                load.wait()
        for j in range(2):
            sib_copy[s][j].wait_recv()
        gate += dot32(xs[s, :, :half], wg[1])
        up += dot32(xs[s, :, :half], wu[1])
        hid_out[s] = (gate / (f32(1.0) + jnp.exp(-gate)) * up).astype(bf16)

    hid_copy = [remote(hid_out.at[s], hid_in.at[s], hid_sem, s, x_peer) for s in range(2)]
    for load in loads[:2]:
        load.wait()
    front(0)
    go(hid_copy[0])
    for i in range(nz):
        d_land[i].wait_recv()
    go(sib_copy[1][1])
    front(1)
    go(hid_copy[1])

    for load in loads[4:]:
        load.wait()
    part_copy = [remote(part_out.at[s], part_in.at[s], part_sem, s, sibling) for s in range(2)]
    lanes = lax.broadcasted_iota(jnp.int32, (2 * column, LANES), 1)
    wanted = (lanes % experts == 2 * p + y) & (lanes < 3 * experts)

    def ret_copy(s, j, i):
        to = dev((ox if j else x), (oy if s else y), (z + nz - i) % nz, c)
        slot = (s * 2 + j) * nz + i
        return remote(ret_out.at[s, spot(ox if j else x, i), :], ret_in.at[slot], ret_sem, slot, to)

    def back(s):
        weight = jnp.sum(jnp.where(wanted, xm[s, :, half:].astype(f32), f32(0.0)), axis=1, keepdims=True)
        hid_copy[s].wait_recv()

        def quarter_of(which):
            cols = pl.ds(pl.multiple_of(which * quarter, quarter), quarter)
            return (dot32(hid_out[s], wd[0, :, cols]) + dot32(hid_in[s], wd[1, :, cols])) * weight

        part_out[s] = quarter_of(oc).astype(bf16)
        go(part_copy[s])
        own = quarter_of(c)
        part_copy[s].wait_recv()
        ret_out[s] = (own + part_in[s].astype(f32)).astype(bf16)
        for i in (2, 1, 3, 0) if nz == 4 else range(nz):
            for j in (1, 0):
                if s or j or i:
                    go(ret_copy(s, j, i))

    back(0)
    back(1)

    sums = [jnp.zeros((block, quarter), f32), jnp.zeros((block, quarter), f32)]
    sums[0] += ret_out[0, spot(x, 0), :].astype(f32)
    for s in range(2):
        for i in range(nz):
            for j in range(2):
                if s or j or i:
                    ret_copy(s, j, i).wait_recv()
                    sums[j] += ret_in[(s * 2 + j) * nz + i].astype(f32)
    for j in range(2):
        fin_out[:, j * quarter : (j + 1) * quarter] = jnp.where(first, sums[j][rows:], sums[j][:rows])
    fin = go(remote(fin_out, fin_in, fin_sem, 0, sibling))
    mine = [jnp.where(first, sums[j][:rows], sums[j][rows:]) for j in range(2)]
    fin.wait_recv()
    other = [fin_in[:, j * quarter : (j + 1) * quarter] for j in range(2)]
    pieces = []
    for h in range(2):
        for q in range(2):
            near = jnp.where(c == q, mine[0], other[0])
            far = jnp.where(c == q, mine[1], other[1])
            pieces.append(jnp.where(x == h, near, far))
    mixed = tok_ref[...].astype(f32) + jnp.concatenate(pieces, axis=1)
    factor = lax.rsqrt(jnp.mean(mixed * mixed, axis=1, keepdims=True) + 1e-06)
    out_ref[...] = (mixed * factor * gain_ref[...]).astype(bf16)
    for copy in sends:
        copy.wait_send()


def fused(tokens, expert_ids, gate_weights, w_gate, w_up, w_down, norm_gain):
    f32, bf16 = jnp.float32, jnp.bfloat16
    rows, width = tokens.shape
    n_ep = lax.axis_size("ep")
    nz, experts = n_ep // 2, 2 * n_ep
    half, quarter = width // 2, width // 4
    block = 2 * rows
    stage = 2 * nz * block
    wide = half + LANES
    ff_half, out_cols = w_gate.shape[2], w_down.shape[2]
    vmem = pltpu.VMEM

    def sems(count):
        return pltpu.SemaphoreType.DMA((2, count))

    whole = pl.BlockSpec(memory_space=pltpu.VMEM)
    return pl.pallas_call(
        functools.partial(fused_kernel, nz, experts),
        out_shape=jax.ShapeDtypeStruct((rows, width), bf16),
        in_specs=[whole] * 4 + [pl.BlockSpec(memory_space=pl.ANY)] * 3,
        out_specs=whole,
        scratch_shapes=[
            vmem((2, half, ff_half), bf16),
            vmem((2, half, ff_half), bf16),
            vmem((2, ff_half, out_cols), bf16),
            vmem((rows, wide), f32),
            vmem((rows, wide), f32),
            vmem((2, stage, wide), bf16),
            vmem((2, stage, wide), bf16),
            vmem((2, stage, ff_half), bf16),
            vmem((2, stage, ff_half), bf16),
            vmem((2, stage, quarter), bf16),
            vmem((2, stage, quarter), bf16),
            vmem((2, stage, quarter), bf16),
            vmem((4 * nz, block, quarter), bf16),
            vmem((rows, half), f32),
            vmem((rows, half), f32),
            pltpu.SemaphoreType.DMA((6,)),
            sems(1), sems(nz), sems(nz), sems(nz), sems(nz), sems(nz), sems(4), sems(2), sems(2),
            sems(4 * nz), sems(1),
        ],
        compiler_params=pltpu.CompilerParams(
            collective_id=0, has_side_effects=True, vmem_limit_bytes=48 * 1024 * 1024
        ),
    )(tokens, expert_ids, gate_weights, norm_gain.reshape(1, width), w_gate, w_up, w_down)


def swapped(shard, axis, bit):
    return lax.ppermute(shard, axis, [(i, i ^ 1 << bit) for i in range(lax.axis_size(axis))])


def expert_front(arrived, gate_slice, up_slice):
    gate_part = jnp.einsum("abmd,df->abmf", arrived, gate_slice, preferred_element_type=jnp.float32)
    up_part = jnp.einsum("abmd,df->abmf", arrived, up_slice, preferred_element_type=jnp.float32)
    return (jax.nn.silu(gate_part) * up_part).astype(jnp.bfloat16)


def routed(tokens, expert_ids, gate_weights, w_gate, w_up, w_down, norm_gain):
    tok_rows, width = tokens.shape
    top_count = expert_ids.shape[1]
    n_ep = lax.axis_size("ep")
    n_grp = lax.axis_size("grp")
    experts = 2 * n_ep
    capacity = max(2, 2 * tok_rows * top_count // experts)
    slots = experts * capacity
    span = n_grp // 2
    flat_ids = expert_ids.reshape(-1)
    onehot = (flat_ids[:, None] == jnp.arange(experts, dtype=jnp.int32)[None, :]).astype(jnp.int32)
    earlier = jnp.cumsum(onehot, axis=0) - onehot
    ranking = jnp.sum(earlier * onehot, axis=1)
    slot_ids = jnp.arange(slots, dtype=jnp.int32)
    send_slot = flat_ids % 2 * (n_ep * capacity) + flat_ids // 2 * capacity + ranking
    placing = send_slot.reshape(tok_rows, top_count)[None, :, :] == slot_ids[:, None, None]
    placing = jnp.sum(placing.astype(jnp.float32), axis=2).astype(jnp.bfloat16)
    outgoing = jnp.dot(placing, tokens, preferred_element_type=jnp.float32).astype(jnp.bfloat16)
    outgoing = outgoing.reshape(2, n_ep, capacity, width)
    gate_slice = w_gate[0]
    up_slice = w_up[0]
    arrived = lax.all_to_all(outgoing, "ep", split_axis=1, concat_axis=1, tiled=True)
    fanned = jnp.repeat(arrived, span, axis=0)
    hidden = expert_front(
        lax.all_to_all(fanned, "grp", split_axis=0, concat_axis=0, tiled=True), gate_slice, up_slice
    )
    my_index = lax.axis_index("grp")
    assembled = hidden
    for level in range(span.bit_length() - 1):
        partner = swapped(assembled, "grp", level)
        upper = my_index // (1 << level) % 2
        assembled = jnp.where(
            upper == 0,
            jnp.concatenate([assembled, partner], axis=3),
            jnp.concatenate([partner, assembled], axis=3),
        )
    expert_out = jnp.einsum(
        "abmf,fc->abmc", assembled, w_down[0], preferred_element_type=jnp.float32
    ).astype(jnp.bfloat16)
    returned = lax.all_to_all(expert_out, "grp", split_axis=0, concat_axis=3, tiled=True)
    returned = returned.reshape(n_ep, capacity, 2, width)
    home = lax.all_to_all(returned, "ep", split_axis=0, concat_axis=0, tiled=True)
    back_slot = flat_ids // 2 * (capacity * 2) + ranking * 2 + flat_ids % 2
    matches = back_slot.reshape(tok_rows, top_count)[:, :, None] == slot_ids[None, None, :]
    weight_table = jnp.sum(jnp.where(matches, gate_weights[:, :, None], jnp.float32(0.0)), axis=1)
    combined = jnp.dot(
        weight_table,
        home.reshape(slots, width).astype(jnp.float32),
        precision=lax.Precision.HIGHEST,
    )
    mixed = tokens.astype(jnp.float32) + combined
    factor = lax.rsqrt(jnp.mean(mixed * mixed, axis=1, keepdims=True) + 1e-06)
    return (mixed * factor * norm_gain).astype(jnp.bfloat16)


def shards(tokens, *rest):
    all_rows = tokens.shape[0] * lax.axis_size("grp") * lax.axis_size("ep")
    dense = lax.axis_size("grp") == 4 and lax.axis_size("ep") % 2 == 0 and all_rows <= 256
    return (fused if dense else routed)(tokens, *rest)


def solution(mesh):
    placed = (
        P(("grp", "ep"), None),
        P(("grp", "ep"), None),
        P(("grp", "ep"), None),
        P("ep", None, "grp"),
        P("ep", None, "grp"),
        P("ep", None, "grp"),
        P(),
    )
    return jax.shard_map(
        shards, mesh=mesh, in_specs=placed, out_specs=P(("grp", "ep"), None), check_vma=False
    )
```

```python
import functools

import jax
import jax.numpy as jnp
from jax import lax
from jax.experimental import pallas as pl
from jax.experimental.pallas import tpu as pltpu
from jax.sharding import PartitionSpec as P

LANES = 128
MESH = pl.DeviceIdType.MESH


def dot32(a, b):
    return jnp.dot(a, b, preferred_element_type=jnp.float32)


def fused_kernel(
    nz, experts,
    tok_hbm, ids_hbm, gates_hbm, gain_hbm, wg_hbm, wu_hbm, wd_hbm, out_ref,
    tok_ref, ids_ref, gates_ref, gain_ref, wg, wu, wd, s_out, s_in, xm, xs, hid_out, hid_in, part_out, part_in, ret_out, ret_in, fin_out, fin_in,
    t_sem, w_sem, s_sem, z_sem, x_sem, y_sem, dx_sem, dy_sem, sib_sem, hid_sem, part_sem, ret_sem, fin_sem,
):
    f32, bf16 = jnp.float32, jnp.bfloat16
    rows, width = tok_ref.shape
    half = width // 2
    quarter = width // 4
    block = 2 * rows
    stage = 2 * nz * block
    piece = quarter // 2
    ff_half = wg.shape[2]
    g, p = lax.axis_index("grp"), lax.axis_index("ep")
    y, x = g // 2, g % 2
    z, c = p // 2, p % 2
    ox, oy, oc = 1 - x, 1 - y, 1 - c

    def dev(xx, yy, zz, cc):
        return (yy * 2 + xx, zz * 2 + cc)

    def remote(src, dst, sems, idx, to):
        return pltpu.make_async_remote_copy(
            src_ref=src, dst_ref=dst, send_sem=sems.at[0, idx], recv_sem=sems.at[1, idx],
            device_id=to, device_id_type=MESH,
        )

    sibling = dev(x, y, z, oc)
    x_peer = dev(ox, y, z, c)
    y_peer = dev(x, oy, z, c)
    x_sibling = dev(ox, y, z, oc)

    small = [
        pltpu.make_async_copy(src, dst, t_sem.at[n])
        for n, (src, dst) in enumerate(
            ((tok_hbm, tok_ref), (ids_hbm, ids_ref), (gates_hbm, gates_ref), (gain_hbm, gain_ref))
        )
    ]
    for load in small:
        load.start()

    loads = []
    n = 0
    for mine, at_k in ((0, c), (1, oc)):
        for src, dst in ((wg_hbm, wg), (wu_hbm, wu)):
            span = pl.ds(pl.multiple_of(at_k * half, half), half)
            loads.append(pltpu.make_async_copy(src.at[0, span, :], dst.at[mine], w_sem.at[n]))
            n += 1
    for mine, at_k in ((0, x), (1, ox)):
        span = pl.ds(pl.multiple_of(at_k * ff_half, ff_half), ff_half)
        loads.append(pltpu.make_async_copy(wd_hbm.at[0, span, :], wd.at[mine], w_sem.at[n]))
        n += 1

    barrier = pltpu.get_barrier_semaphore()
    greeted = 0
    for to in [dev(x, (y + dy) % 2, (z + dz) % nz, c) for dy in range(2) for dz in range(nz) if dy or dz] + [
        x_peer, sibling, x_sibling
    ]:
        pl.semaphore_signal(barrier, inc=1, device_id=to, device_id_type=MESH)
        greeted += 1
    for load in small:
        load.wait()
    for load in loads:
        load.start()

    lane = lax.broadcasted_iota(jnp.int32, (rows, LANES), 1)
    table = jnp.zeros((rows, LANES), f32)
    for k in range(ids_ref.shape[1]):
        table += jnp.where(ids_ref[:, k : k + 1] == lane % experts, gates_ref[:, k : k + 1], f32(0.0))
    tok = tok_ref[...].astype(f32)
    first = c == 0
    mine_half = jnp.where(first, tok[:, :half], tok[:, half:])
    s_out[:, :half] = jnp.where(first, tok[:, half:], tok[:, :half])
    s_out[:, half:] = table
    pl.semaphore_wait(barrier, greeted)

    sends = []

    def go(copy):
        copy.start()
        sends.append(copy)
        return copy

    swap = go(remote(s_out, s_in, s_sem, 0, sibling))
    swap.wait_recv()
    theirs, their_table = s_in[:, :half], s_in[:, half:]

    def both(a, b):
        return jnp.where(first, jnp.concatenate([a, b], axis=0), jnp.concatenate([b, a], axis=0))

    pair_table = both(table, their_table)
    high = pair_table.astype(bf16)
    rest = pair_table - high.astype(f32)
    middle = rest.astype(bf16)
    low = (rest - middle.astype(f32)).astype(bf16)
    part = lax.broadcasted_iota(jnp.int32, (block, LANES), 1) // experts
    coded = jnp.where(
        part == 0, high.astype(f32),
        jnp.where(part == 1, middle.astype(f32), jnp.where(part == 2, low.astype(f32), f32(0.0))),
    )

    def spot(xx, i):
        return pl.ds(pl.multiple_of((2 * i + xx) * block, block), block)

    def pair(i):
        return slice(2 * i * block, 2 * (i + 1) * block)

    xm[0, spot(x, 0), :] = jnp.concatenate([both(mine_half, theirs), coded], axis=1).astype(bf16)

    z_copy = [None] + [
        remote(xm.at[0, spot(x, 0), :], xm.at[0, spot(x, i), :], z_sem, i, dev(x, y, (z + i) % nz, c))
        for i in range(1, nz)
    ]
    x_copy = [remote(xm.at[0, spot(x, i), :], xm.at[0, spot(x, i), :], x_sem, i, x_peer) for i in range(nz)]
    x_land = [remote(xm.at[0, spot(ox, i), :], xm.at[0, spot(ox, i), :], x_sem, i, x_peer) for i in range(nz)]
    y_copy = [remote(xm.at[0, spot(x, i), :], xm.at[1, spot(x, i), :], y_sem, i, y_peer) for i in range(nz)]
    by_y = [i for i in range(nz) if i % 4 in (1, 2)]
    d_copy, d_land = [], []
    for i in range(nz):
        if i in by_y:
            d_copy.append(remote(xm.at[0, spot(ox, i), :], xm.at[1, spot(ox, i), :], dy_sem, i, y_peer))
            d_land.append(d_copy[-1])
        else:
            d_copy.append(remote(xm.at[1, spot(x, i), :], xm.at[1, spot(x, i), :], dx_sem, i, x_peer))
            d_land.append(remote(xm.at[1, spot(ox, i), :], xm.at[1, spot(ox, i), :], dx_sem, i, x_peer))
    sib_copy = [
        [remote(xm.at[s, pair(i), :], xs.at[s, pair(i), :], sib_sem, s * nz + i, sibling) for i in range(nz)]
        for s in range(2)
    ]

    for i in range(1, nz):
        go(z_copy[i])
    go(x_copy[0])
    go(y_copy[0])
    for i in range(nz):
        if i + 1 < nz:
            z_copy[i + 1].wait_recv()
            go(x_copy[i + 1])
            go(y_copy[i + 1])
        x_land[i].wait_recv()
        if i in by_y:
            go(d_copy[i])
        go(sib_copy[0][i])
        y_copy[i].wait_recv()
        if i not in by_y:
            go(d_copy[i])

    def front(s):
        gate = dot32(xm[s, :, :half], wg[0])
        up = dot32(xm[s, :, :half], wu[0])
        if s == 0:
            for load in loads[2:4]:
                load.wait()
        for i in range(nz):
            sib_copy[s][i].wait_recv()
        gate += dot32(xs[s, :, :half], wg[1])
        up += dot32(xs[s, :, :half], wu[1])
        hid_out[s] = (gate / (f32(1.0) + jnp.exp(-gate)) * up).astype(bf16)

    hid_copy = [remote(hid_out.at[s], hid_in.at[s], hid_sem, s, x_peer) for s in range(2)]
    for load in loads[:2]:
        load.wait()
    front(0)
    go(hid_copy[0])
    for i in range(nz):
        d_land[i].wait_recv()
        go(sib_copy[1][i])
    front(1)
    go(hid_copy[1])

    for load in loads[4:]:
        load.wait()
    part_copy = [
        [remote(part_out.at[s, e], part_in.at[s, e], part_sem, 2 * s + e, sibling) for e in range(2)]
        for s in range(2)
    ]
    lanes = lax.broadcasted_iota(jnp.int32, (stage, LANES), 1)
    wanted = (lanes % experts == 2 * p + y) & (lanes < 3 * experts)

    def ret_copy(s, e, i):
        to = dev(x, (oy if s else y), (z + nz - i) % nz, c)
        slot = (s * 2 + e) * nz + i
        return remote(ret_out.at[s, e, pair(i), :], ret_in.at[slot], ret_sem, slot, to)

    def back(s):
        weight = jnp.sum(jnp.where(wanted, xm[s, :, half:].astype(f32), f32(0.0)), axis=1, keepdims=True)
        hid_copy[s].wait_recv()

        def piece_of(which, e):
            cols = pl.ds(pl.multiple_of(which * quarter + e * piece, piece), piece)
            return (dot32(hid_out[s], wd[0, :, cols]) + dot32(hid_in[s], wd[1, :, cols])) * weight

        for e in range(2):
            part_out[s, e] = piece_of(oc, e).astype(bf16)
            go(part_copy[s][e])
        for e in range(2):
            own = piece_of(c, e)
            part_copy[s][e].wait_recv()
            ret_out[s, e] = (own + part_in[s, e].astype(f32)).astype(bf16)
            for i in (2, 1, 3, 0) if nz == 4 else range(nz):
                if s or i:
                    go(ret_copy(s, e, i))

    back(0)
    back(1)

    for e in range(2):
        total = ret_out[0, e, pair(0), :].astype(f32)
        for s in range(2):
            for i in range(nz):
                if s or i:
                    ret_copy(s, e, i).wait_recv()
                    total += ret_in[(s * 2 + e) * nz + i].astype(f32)
        fin_out[:, e * piece : (e + 1) * piece] = total

    def rows_of(xx, cc):
        return pl.ds(pl.multiple_of((xx * 2 + cc) * rows, rows), rows)

    fin_copy = [
        remote(fin_out.at[rows_of(xx, cc), :], fin_in.at[n], fin_sem, n, to)
        for n, (xx, cc, to) in enumerate(((ox, c, x_peer), (ox, oc, x_sibling), (x, oc, sibling)))
    ]
    for copy in fin_copy:
        go(copy)
    kept = fin_out[rows_of(x, c), :]
    for copy in fin_copy:
        copy.wait_recv()
    pieces = []
    for h in range(2):
        for q in range(2):
            near = jnp.where(c == q, kept, fin_in[2])
            far = jnp.where(c == q, fin_in[0], fin_in[1])
            pieces.append(jnp.where(x == h, near, far))
    mixed = tok + jnp.concatenate(pieces, axis=1)
    factor = lax.rsqrt(jnp.mean(mixed * mixed, axis=1, keepdims=True) + 1e-06)
    out_ref[...] = (mixed * factor * gain_ref[...]).astype(bf16)
    for copy in sends:
        copy.wait_send()


def fused(tokens, expert_ids, gate_weights, w_gate, w_up, w_down, norm_gain):
    f32, bf16 = jnp.float32, jnp.bfloat16
    rows, width = tokens.shape
    n_ep = lax.axis_size("ep")
    nz, experts = n_ep // 2, 2 * n_ep
    half, quarter = width // 2, width // 4
    block = 2 * rows
    stage = 2 * nz * block
    wide = half + LANES
    ff_half, out_cols = w_gate.shape[2], w_down.shape[2]
    vmem = pltpu.VMEM

    def sems(count):
        return pltpu.SemaphoreType.DMA((2, count))

    return pl.pallas_call(
        functools.partial(fused_kernel, nz, experts),
        out_shape=jax.ShapeDtypeStruct((rows, width), bf16),
        in_specs=[pl.BlockSpec(memory_space=pltpu.HBM)] * 7,
        out_specs=pl.BlockSpec(memory_space=pltpu.VMEM),
        scratch_shapes=[
            vmem((rows, width), bf16),
            vmem(expert_ids.shape, jnp.int32),
            vmem(gate_weights.shape, f32),
            vmem((1, width), f32),
            vmem((2, half, ff_half), bf16),
            vmem((2, half, ff_half), bf16),
            vmem((2, ff_half, out_cols), bf16),
            vmem((rows, wide), f32),
            vmem((rows, wide), f32),
            vmem((2, stage, wide), bf16),
            vmem((2, stage, wide), bf16),
            vmem((2, stage, ff_half), bf16),
            vmem((2, stage, ff_half), bf16),
            vmem((2, 2, stage, quarter // 2), bf16),
            vmem((2, 2, stage, quarter // 2), bf16),
            vmem((2, 2, stage, quarter // 2), bf16),
            vmem((4 * nz, 2 * block, quarter // 2), bf16),
            vmem((2 * block, quarter), f32),
            vmem((3, rows, quarter), f32),
            pltpu.SemaphoreType.DMA((4,)),
            pltpu.SemaphoreType.DMA((6,)),
            sems(1), sems(nz), sems(nz), sems(nz), sems(nz), sems(nz), sems(2 * nz), sems(2), sems(4),
            sems(4 * nz), sems(3),
        ],
        compiler_params=pltpu.CompilerParams(
            collective_id=0, has_side_effects=True, vmem_limit_bytes=56 * 1024 * 1024
        ),
    )(tokens, expert_ids, gate_weights, norm_gain.reshape(1, width), w_gate, w_up, w_down)


def swapped(shard, axis, bit):
    return lax.ppermute(shard, axis, [(i, i ^ 1 << bit) for i in range(lax.axis_size(axis))])


def expert_front(arrived, gate_slice, up_slice):
    gate_part = jnp.einsum("abmd,df->abmf", arrived, gate_slice, preferred_element_type=jnp.float32)
    up_part = jnp.einsum("abmd,df->abmf", arrived, up_slice, preferred_element_type=jnp.float32)
    return (jax.nn.silu(gate_part) * up_part).astype(jnp.bfloat16)


def routed(tokens, expert_ids, gate_weights, w_gate, w_up, w_down, norm_gain):
    tok_rows, width = tokens.shape
    top_count = expert_ids.shape[1]
    n_ep = lax.axis_size("ep")
    n_grp = lax.axis_size("grp")
    experts = 2 * n_ep
    capacity = max(2, 2 * tok_rows * top_count // experts)
    slots = experts * capacity
    span = n_grp // 2
    flat_ids = expert_ids.reshape(-1)
    onehot = (flat_ids[:, None] == jnp.arange(experts, dtype=jnp.int32)[None, :]).astype(jnp.int32)
    earlier = jnp.cumsum(onehot, axis=0) - onehot
    ranking = jnp.sum(earlier * onehot, axis=1)
    slot_ids = jnp.arange(slots, dtype=jnp.int32)
    send_slot = flat_ids % 2 * (n_ep * capacity) + flat_ids // 2 * capacity + ranking
    placing = send_slot.reshape(tok_rows, top_count)[None, :, :] == slot_ids[:, None, None]
    placing = jnp.sum(placing.astype(jnp.float32), axis=2).astype(jnp.bfloat16)
    outgoing = jnp.dot(placing, tokens, preferred_element_type=jnp.float32).astype(jnp.bfloat16)
    outgoing = outgoing.reshape(2, n_ep, capacity, width)
    gate_slice = w_gate[0]
    up_slice = w_up[0]
    arrived = lax.all_to_all(outgoing, "ep", split_axis=1, concat_axis=1, tiled=True)
    fanned = jnp.repeat(arrived, span, axis=0)
    hidden = expert_front(
        lax.all_to_all(fanned, "grp", split_axis=0, concat_axis=0, tiled=True), gate_slice, up_slice
    )
    my_index = lax.axis_index("grp")
    assembled = hidden
    for level in range(span.bit_length() - 1):
        partner = swapped(assembled, "grp", level)
        upper = my_index // (1 << level) % 2
        assembled = jnp.where(
            upper == 0,
            jnp.concatenate([assembled, partner], axis=3),
            jnp.concatenate([partner, assembled], axis=3),
        )
    expert_out = jnp.einsum(
        "abmf,fc->abmc", assembled, w_down[0], preferred_element_type=jnp.float32
    ).astype(jnp.bfloat16)
    returned = lax.all_to_all(expert_out, "grp", split_axis=0, concat_axis=3, tiled=True)
    returned = returned.reshape(n_ep, capacity, 2, width)
    home = lax.all_to_all(returned, "ep", split_axis=0, concat_axis=0, tiled=True)
    back_slot = flat_ids // 2 * (capacity * 2) + ranking * 2 + flat_ids % 2
    matches = back_slot.reshape(tok_rows, top_count)[:, :, None] == slot_ids[None, None, :]
    weight_table = jnp.sum(jnp.where(matches, gate_weights[:, :, None], jnp.float32(0.0)), axis=1)
    combined = jnp.dot(
        weight_table,
        home.reshape(slots, width).astype(jnp.float32),
        precision=lax.Precision.HIGHEST,
    )
    mixed = tokens.astype(jnp.float32) + combined
    factor = lax.rsqrt(jnp.mean(mixed * mixed, axis=1, keepdims=True) + 1e-06)
    return (mixed * factor * norm_gain).astype(jnp.bfloat16)


def shards(tokens, *rest):
    all_rows = tokens.shape[0] * lax.axis_size("grp") * lax.axis_size("ep")
    dense = lax.axis_size("grp") == 4 and lax.axis_size("ep") % 2 == 0 and all_rows <= 256
    return (fused if dense else routed)(tokens, *rest)


def solution(mesh):
    placed = (
        P(("grp", "ep"), None),
        P(("grp", "ep"), None),
        P(("grp", "ep"), None),
        P("ep", None, "grp"),
        P("ep", None, "grp"),
        P("ep", None, "grp"),
        P(),
    )
    return jax.shard_map(
        shards, mesh=mesh, in_specs=placed, out_specs=P(("grp", "ep"), None), check_vma=False
    )
```

```python
import functools

import jax
import jax.numpy as jnp
from jax import lax
from jax.experimental import pallas as pl
from jax.experimental.pallas import tpu as pltpu
from jax.sharding import PartitionSpec as P

LANES = 128
MESH = pl.DeviceIdType.MESH


def dot32(a, b):
    return jnp.dot(a, b, preferred_element_type=jnp.float32)


def fused_kernel(
    nz, experts,
    tok_hbm, ids_hbm, gates_hbm, gain_hbm, wg_hbm, wu_hbm, wd_hbm, out_ref,
    tok_ref, ids_ref, gates_ref, gain_ref, wg, wu, wd, s_out, s_in, xm, xs, hid_out, hid_in, part_out, part_in, ret_out, ret_in, fin_out, fin_in,
    t_sem, w_sem, s_sem, z_sem, x_sem, y_sem, dx_sem, dy_sem, sib_sem, hid_sem, part_sem, ret_sem, fin_sem,
):
    f32, bf16 = jnp.float32, jnp.bfloat16
    rows, width = tok_ref.shape
    half = width // 2
    quarter = width // 4
    block = 2 * rows
    stage = 2 * nz * block
    piece = quarter // 2
    ff_half = wg.shape[2]
    ff_part = ff_half // 2
    g, p = lax.axis_index("grp"), lax.axis_index("ep")
    y, x = g // 2, g % 2
    z, c = p // 2, p % 2
    ox, oy, oc = 1 - x, 1 - y, 1 - c

    def dev(xx, yy, zz, cc):
        return (yy * 2 + xx, zz * 2 + cc)

    def along(i):
        return (z // 2 * 2 + (z + i) % 2 + i // 2 * 2) % nz

    def remote(src, dst, sems, idx, to):
        return pltpu.make_async_remote_copy(
            src_ref=src, dst_ref=dst, send_sem=sems.at[0, idx], recv_sem=sems.at[1, idx],
            device_id=to, device_id_type=MESH,
        )

    sibling = dev(x, y, z, oc)
    x_peer = dev(ox, y, z, c)
    y_peer = dev(x, oy, z, c)
    x_sibling = dev(ox, y, z, oc)

    small = [
        pltpu.make_async_copy(src, dst, t_sem.at[n])
        for n, (src, dst) in enumerate(
            ((tok_hbm, tok_ref), (ids_hbm, ids_ref), (gates_hbm, gates_ref), (gain_hbm, gain_ref))
        )
    ]
    for load in small:
        load.start()

    loads = []
    n = 0
    for mine, at_k in ((0, c), (1, oc)):
        for src, dst in ((wg_hbm, wg), (wu_hbm, wu)):
            span = pl.ds(pl.multiple_of(at_k * half, half), half)
            loads.append(pltpu.make_async_copy(src.at[0, span, :], dst.at[mine], w_sem.at[n]))
            n += 1
    for mine, at_k in ((0, x), (1, ox)):
        span = pl.ds(pl.multiple_of(at_k * ff_half, ff_half), ff_half)
        loads.append(pltpu.make_async_copy(wd_hbm.at[0, span, :], wd.at[mine], w_sem.at[n]))
        n += 1

    barrier = pltpu.get_barrier_semaphore()
    greeted = 0
    for to in [dev(x, (y + dy) % 2, (z + dz) % nz, c) for dy in range(2) for dz in range(nz) if dy or dz] + [
        x_peer, sibling, x_sibling
    ]:
        pl.semaphore_signal(barrier, inc=1, device_id=to, device_id_type=MESH)
        greeted += 1
    for load in small:
        load.wait()
    for load in loads:
        load.start()

    lane = lax.broadcasted_iota(jnp.int32, (rows, LANES), 1)
    table = jnp.zeros((rows, LANES), f32)
    for k in range(ids_ref.shape[1]):
        table += jnp.where(ids_ref[:, k : k + 1] == lane % experts, gates_ref[:, k : k + 1], f32(0.0))
    tok = tok_ref[...].astype(f32)
    first = c == 0
    mine_half = jnp.where(first, tok[:, :half], tok[:, half:])
    s_out[:, :half] = jnp.where(first, tok[:, half:], tok[:, :half])
    s_out[:, half:] = table
    pl.semaphore_wait(barrier, greeted)

    sends = []

    def go(copy):
        copy.start()
        sends.append(copy)
        return copy

    swap = go(remote(s_out, s_in, s_sem, 0, sibling))
    swap.wait_recv()
    theirs, their_table = s_in[:, :half], s_in[:, half:]

    def both(a, b):
        return jnp.where(first, jnp.concatenate([a, b], axis=0), jnp.concatenate([b, a], axis=0))

    pair_table = both(table, their_table)
    high = pair_table.astype(bf16)
    rest = pair_table - high.astype(f32)
    middle = rest.astype(bf16)
    low = (rest - middle.astype(f32)).astype(bf16)
    part = lax.broadcasted_iota(jnp.int32, (block, LANES), 1) // experts
    coded = jnp.where(
        part == 0, high.astype(f32),
        jnp.where(part == 1, middle.astype(f32), jnp.where(part == 2, low.astype(f32), f32(0.0))),
    )

    def spot(xx, i):
        return pl.ds(pl.multiple_of((2 * i + xx) * block, block), block)

    def pair(i):
        return slice(2 * i * block, 2 * (i + 1) * block)

    xm[0, spot(x, 0), :] = jnp.concatenate([both(mine_half, theirs), coded], axis=1).astype(bf16)

    z_copy = [None] + [
        remote(xm.at[0, spot(x, 0), :], xm.at[0, spot(x, i), :], z_sem, i, dev(x, y, along(i), c))
        for i in range(1, nz)
    ]
    x_copy = [remote(xm.at[0, spot(x, i), :], xm.at[0, spot(x, i), :], x_sem, i, x_peer) for i in range(nz)]
    x_land = [remote(xm.at[0, spot(ox, i), :], xm.at[0, spot(ox, i), :], x_sem, i, x_peer) for i in range(nz)]
    y_copy = [remote(xm.at[0, spot(x, i), :], xm.at[1, spot(x, i), :], y_sem, i, y_peer) for i in range(nz)]
    by_y = [i for i in range(nz) if i % 4 in (1, 2)]
    d_copy, d_land = [], []
    for i in range(nz):
        if i in by_y:
            d_copy.append(remote(xm.at[0, spot(ox, i), :], xm.at[1, spot(ox, i), :], dy_sem, i, y_peer))
            d_land.append(d_copy[-1])
        else:
            d_copy.append(remote(xm.at[1, spot(x, i), :], xm.at[1, spot(x, i), :], dx_sem, i, x_peer))
            d_land.append(remote(xm.at[1, spot(ox, i), :], xm.at[1, spot(ox, i), :], dx_sem, i, x_peer))
    sib_copy = [
        [remote(xm.at[s, pair(i), :], xs.at[s, pair(i), :], sib_sem, s * nz + i, sibling) for i in range(nz)]
        for s in range(2)
    ]

    for i in range(1, nz):
        go(z_copy[i])
    go(x_copy[0])
    go(y_copy[0])
    for i in range(nz):
        if i + 1 < nz:
            z_copy[i + 1].wait_recv()
            go(x_copy[i + 1])
            go(y_copy[i + 1])
        x_land[i].wait_recv()
        if i in by_y:
            go(d_copy[i])
        go(sib_copy[0][i])
        y_copy[i].wait_recv()
        if i not in by_y:
            go(d_copy[i])

    def hid_copy(s, n):
        return remote(hid_out.at[s, n], hid_in.at[s, n], hid_sem, 2 * s + n, x_peer)

    def front(s):
        for i in range(nz):
            sib_copy[s][i].wait_recv()

        @pl.loop(0, 2)
        def _(n):
            cols = pl.ds(pl.multiple_of(n * ff_part, ff_part), ff_part)
            gate = dot32(xm[s, :, :half], wg[0, :, cols]) + dot32(xs[s, :, :half], wg[1, :, cols])
            up = dot32(xm[s, :, :half], wu[0, :, cols]) + dot32(xs[s, :, :half], wu[1, :, cols])
            hid_out[s, n] = (gate / (f32(1.0) + jnp.exp(-gate)) * up).astype(bf16)
            hid_copy(s, n).start()

    for load in loads[:4]:
        load.wait()
    front(0)
    for i in range(nz):
        d_land[i].wait_recv()
        go(sib_copy[1][i])
    front(1)

    for load in loads[4:]:
        load.wait()
    def part_copy(s, e):
        return remote(part_out.at[s, e], part_in.at[s, e], part_sem, 2 * s + e, sibling)

    lanes = lax.broadcasted_iota(jnp.int32, (stage, LANES), 1)
    wanted = (lanes % experts == 2 * p + y) & (lanes < 3 * experts)

    def ret_copy(s, e, i):
        to = dev(x, (oy if s else y), along(i), c)
        slot = (s * 2 + e) * nz + i
        return remote(ret_out.at[s, e, pair(i), :], ret_in.at[slot], ret_sem, slot, to)

    def back(s):
        weight = jnp.sum(jnp.where(wanted, xm[s, :, half:].astype(f32), f32(0.0)), axis=1, keepdims=True)
        for n in range(2):
            hid_copy(s, n).wait_recv()

        def piece_of(which, e):
            cols = pl.ds(pl.multiple_of(which * quarter + e * piece, piece), piece)
            total = jnp.zeros((stage, piece), f32)
            for n in range(2):
                span = slice(n * ff_part, (n + 1) * ff_part)
                total += dot32(hid_out[s, n], wd[0, span, cols]) + dot32(hid_in[s, n], wd[1, span, cols])
            return total * weight

        @pl.loop(0, 2)
        def _(e):
            part_out[s, e] = piece_of(oc, e).astype(bf16)
            part_copy(s, e).start()

        @pl.loop(0, 2)
        def _(e):
            own = piece_of(c, e)
            part_copy(s, e).wait_recv()
            ret_out[s, e] = (own + part_in[s, e].astype(f32)).astype(bf16)
            for i in reversed(range(nz)):
                if s or i:
                    ret_copy(s, e, i).start()

    back(0)
    back(1)

    for e in range(2):
        total = ret_out[0, e, pair(0), :].astype(f32)
        for s in range(2):
            for i in range(nz):
                if s or i:
                    ret_copy(s, e, i).wait_recv()
                    total += ret_in[(s * 2 + e) * nz + i].astype(f32)
        fin_out[:, e * piece : (e + 1) * piece] = total

    def rows_of(xx, cc):
        return pl.ds(pl.multiple_of((xx * 2 + cc) * rows, rows), rows)

    fin_copy = [
        remote(fin_out.at[rows_of(xx, cc), :], fin_in.at[n], fin_sem, n, to)
        for n, (xx, cc, to) in enumerate(((ox, c, x_peer), (ox, oc, x_sibling), (x, oc, sibling)))
    ]
    for copy in fin_copy:
        go(copy)
    kept = fin_out[rows_of(x, c), :]
    for copy in fin_copy:
        copy.wait_recv()
    pieces = []
    for h in range(2):
        for q in range(2):
            near = jnp.where(c == q, kept, fin_in[2])
            far = jnp.where(c == q, fin_in[0], fin_in[1])
            pieces.append(jnp.where(x == h, near, far))
    mixed = tok + jnp.concatenate(pieces, axis=1)
    factor = lax.rsqrt(jnp.mean(mixed * mixed, axis=1, keepdims=True) + 1e-06)
    out_ref[...] = (mixed * factor * gain_ref[...]).astype(bf16)
    for s in range(2):
        for e in range(2):
            hid_copy(s, e).wait_send()
            part_copy(s, e).wait_send()
            for i in range(nz):
                if s or i:
                    ret_copy(s, e, i).wait_send()
    for copy in sends:
        copy.wait_send()


def fused(tokens, expert_ids, gate_weights, w_gate, w_up, w_down, norm_gain):
    f32, bf16 = jnp.float32, jnp.bfloat16
    rows, width = tokens.shape
    n_ep = lax.axis_size("ep")
    nz, experts = n_ep // 2, 2 * n_ep
    half, quarter = width // 2, width // 4
    block = 2 * rows
    stage = 2 * nz * block
    wide = half + LANES
    ff_half, out_cols = w_gate.shape[2], w_down.shape[2]
    vmem = pltpu.VMEM

    def sems(count):
        return pltpu.SemaphoreType.DMA((2, count))

    return pl.pallas_call(
        functools.partial(fused_kernel, nz, experts),
        out_shape=jax.ShapeDtypeStruct((rows, width), bf16),
        in_specs=[pl.BlockSpec(memory_space=pltpu.HBM)] * 7,
        out_specs=pl.BlockSpec(memory_space=pltpu.VMEM),
        scratch_shapes=[
            vmem((rows, width), bf16),
            vmem(expert_ids.shape, jnp.int32),
            vmem(gate_weights.shape, f32),
            vmem((1, width), f32),
            vmem((2, half, ff_half), bf16),
            vmem((2, half, ff_half), bf16),
            vmem((2, ff_half, out_cols), bf16),
            vmem((rows, wide), f32),
            vmem((rows, wide), f32),
            vmem((2, stage, wide), bf16),
            vmem((2, stage, wide), bf16),
            vmem((2, 2, stage, ff_half // 2), bf16),
            vmem((2, 2, stage, ff_half // 2), bf16),
            vmem((2, 2, stage, quarter // 2), bf16),
            vmem((2, 2, stage, quarter // 2), bf16),
            vmem((2, 2, stage, quarter // 2), bf16),
            vmem((4 * nz, 2 * block, quarter // 2), bf16),
            vmem((2 * block, quarter), f32),
            vmem((3, rows, quarter), f32),
            pltpu.SemaphoreType.DMA((4,)),
            pltpu.SemaphoreType.DMA((6,)),
            sems(1), sems(nz), sems(nz), sems(nz), sems(nz), sems(nz), sems(2 * nz), sems(4), sems(4),
            sems(4 * nz), sems(3),
        ],
        compiler_params=pltpu.CompilerParams(
            collective_id=0, has_side_effects=True, vmem_limit_bytes=56 * 1024 * 1024
        ),
    )(tokens, expert_ids, gate_weights, norm_gain.reshape(1, width), w_gate, w_up, w_down)


def swapped(shard, axis, bit):
    return lax.ppermute(shard, axis, [(i, i ^ 1 << bit) for i in range(lax.axis_size(axis))])


def expert_front(arrived, gate_slice, up_slice):
    gate_part = jnp.einsum("abmd,df->abmf", arrived, gate_slice, preferred_element_type=jnp.float32)
    up_part = jnp.einsum("abmd,df->abmf", arrived, up_slice, preferred_element_type=jnp.float32)
    return (jax.nn.silu(gate_part) * up_part).astype(jnp.bfloat16)


def routed(tokens, expert_ids, gate_weights, w_gate, w_up, w_down, norm_gain):
    tok_rows, width = tokens.shape
    top_count = expert_ids.shape[1]
    n_ep = lax.axis_size("ep")
    n_grp = lax.axis_size("grp")
    experts = 2 * n_ep
    capacity = max(2, 2 * tok_rows * top_count // experts)
    slots = experts * capacity
    span = n_grp // 2
    flat_ids = expert_ids.reshape(-1)
    onehot = (flat_ids[:, None] == jnp.arange(experts, dtype=jnp.int32)[None, :]).astype(jnp.int32)
    earlier = jnp.cumsum(onehot, axis=0) - onehot
    ranking = jnp.sum(earlier * onehot, axis=1)
    slot_ids = jnp.arange(slots, dtype=jnp.int32)
    send_slot = flat_ids % 2 * (n_ep * capacity) + flat_ids // 2 * capacity + ranking
    placing = send_slot.reshape(tok_rows, top_count)[None, :, :] == slot_ids[:, None, None]
    placing = jnp.sum(placing.astype(jnp.float32), axis=2).astype(jnp.bfloat16)
    outgoing = jnp.dot(placing, tokens, preferred_element_type=jnp.float32).astype(jnp.bfloat16)
    outgoing = outgoing.reshape(2, n_ep, capacity, width)
    gate_slice = w_gate[0]
    up_slice = w_up[0]
    arrived = lax.all_to_all(outgoing, "ep", split_axis=1, concat_axis=1, tiled=True)
    fanned = jnp.repeat(arrived, span, axis=0)
    hidden = expert_front(
        lax.all_to_all(fanned, "grp", split_axis=0, concat_axis=0, tiled=True), gate_slice, up_slice
    )
    my_index = lax.axis_index("grp")
    assembled = hidden
    for level in range(span.bit_length() - 1):
        partner = swapped(assembled, "grp", level)
        upper = my_index // (1 << level) % 2
        assembled = jnp.where(
            upper == 0,
            jnp.concatenate([assembled, partner], axis=3),
            jnp.concatenate([partner, assembled], axis=3),
        )
    expert_out = jnp.einsum(
        "abmf,fc->abmc", assembled, w_down[0], preferred_element_type=jnp.float32
    ).astype(jnp.bfloat16)
    returned = lax.all_to_all(expert_out, "grp", split_axis=0, concat_axis=3, tiled=True)
    returned = returned.reshape(n_ep, capacity, 2, width)
    home = lax.all_to_all(returned, "ep", split_axis=0, concat_axis=0, tiled=True)
    back_slot = flat_ids // 2 * (capacity * 2) + ranking * 2 + flat_ids % 2
    matches = back_slot.reshape(tok_rows, top_count)[:, :, None] == slot_ids[None, None, :]
    weight_table = jnp.sum(jnp.where(matches, gate_weights[:, :, None], jnp.float32(0.0)), axis=1)
    combined = jnp.dot(
        weight_table,
        home.reshape(slots, width).astype(jnp.float32),
        precision=lax.Precision.HIGHEST,
    )
    mixed = tokens.astype(jnp.float32) + combined
    factor = lax.rsqrt(jnp.mean(mixed * mixed, axis=1, keepdims=True) + 1e-06)
    return (mixed * factor * norm_gain).astype(jnp.bfloat16)


def shards(tokens, *rest):
    all_rows = tokens.shape[0] * lax.axis_size("grp") * lax.axis_size("ep")
    dense = lax.axis_size("grp") == 4 and lax.axis_size("ep") == 8 and all_rows <= 256
    return (fused if dense else routed)(tokens, *rest)


def solution(mesh):
    placed = (
        P(("grp", "ep"), None),
        P(("grp", "ep"), None),
        P(("grp", "ep"), None),
        P("ep", None, "grp"),
        P("ep", None, "grp"),
        P("ep", None, "grp"),
        P(),
    )
    return jax.shard_map(
        shards, mesh=mesh, in_specs=placed, out_specs=P(("grp", "ep"), None), check_vma=False
    )
```

```python
import functools

import jax
import jax.numpy as jnp
from jax import lax
from jax.experimental import pallas as pl
from jax.experimental.pallas import tpu as pltpu
from jax.sharding import PartitionSpec as P

LANES = 128
MESH = pl.DeviceIdType.MESH


def dot32(a, b):
    return jnp.dot(a, b, preferred_element_type=jnp.float32)


def fused_kernel(
    nz, experts,
    tok_hbm, ids_hbm, gates_hbm, gain_hbm, wg_hbm, wu_hbm, wd_hbm, out_ref,
    tok_ref, ids_ref, gates_ref, gain_ref, wg, wu, wd, xb, lhs, tabs, hid_out, hid_in, part_out, part_in, ret_out, ret_in, fin_out, fin_in,
    t_sem, w_sem, z_sem, x_sem, y_sem, dx_sem, dy_sem, sib_sem, hid_sem, part_sem, ret_sem, fin_sem,
):
    f32, bf16 = jnp.float32, jnp.bfloat16
    rows, width = tok_ref.shape
    half = width // 2
    quarter = width // 4
    block = 2 * rows
    stage = 2 * nz * block
    piece = quarter // 2
    ff_half = wg.shape[2]
    ff_part = ff_half // 2
    g, p = lax.axis_index("grp"), lax.axis_index("ep")
    y, x = g // 2, g % 2
    z, c = p // 2, p % 2
    ox, oy, oc = 1 - x, 1 - y, 1 - c

    def dev(xx, yy, zz, cc):
        return (yy * 2 + xx, zz * 2 + cc)

    def along(i):
        return (z // 2 * 2 + (z + i) % 2 + i // 2 * 2) % nz

    def remote(src, dst, sems, idx, to):
        return pltpu.make_async_remote_copy(
            src_ref=src, dst_ref=dst, send_sem=sems.at[0, idx], recv_sem=sems.at[1, idx],
            device_id=to, device_id_type=MESH,
        )

    sibling = dev(x, y, z, oc)
    x_peer = dev(ox, y, z, c)
    y_peer = dev(x, oy, z, c)
    x_sibling = dev(ox, y, z, oc)

    small = [
        pltpu.make_async_copy(src, dst, t_sem.at[n])
        for n, (src, dst) in enumerate(
            ((tok_hbm, tok_ref), (ids_hbm, ids_ref), (gates_hbm, gates_ref), (gain_hbm, gain_ref))
        )
    ]
    for load in small:
        load.start()

    loads = []
    n = 0
    for k in range(2):
        for src, dst in ((wg_hbm, wg), (wu_hbm, wu)):
            loads.append(pltpu.make_async_copy(src.at[0, pl.ds(k * half, half), :], dst.at[k], w_sem.at[n]))
            n += 1
    for mine, at_k in ((0, x), (1, ox)):
        span = pl.ds(pl.multiple_of(at_k * ff_half, ff_half), ff_half)
        loads.append(pltpu.make_async_copy(wd_hbm.at[0, span, :], wd.at[mine], w_sem.at[n]))
        n += 1

    barrier = pltpu.get_barrier_semaphore()
    greeted = 0
    for to in [dev(x, (y + dy) % 2, (z + dz) % nz, c) for dy in range(2) for dz in range(nz) if dy or dz] + [
        x_peer, sibling, x_sibling
    ]:
        pl.semaphore_signal(barrier, inc=1, device_id=to, device_id_type=MESH)
        greeted += 1
    for load in small:
        load.wait()
    for load in loads:
        load.start()

    lane = lax.broadcasted_iota(jnp.int32, (rows, LANES), 1)
    table = jnp.zeros((rows, LANES), f32)
    for k in range(ids_ref.shape[1]):
        table += jnp.where(ids_ref[:, k : k + 1] == lane % experts, gates_ref[:, k : k + 1], f32(0.0))
    tok = tok_ref[...].astype(f32)
    high = table.astype(bf16)
    rest = table - high.astype(f32)
    middle = rest.astype(bf16)
    low = (rest - middle.astype(f32)).astype(bf16)
    part = lane // experts
    coded = jnp.where(
        part == 0, high.astype(f32),
        jnp.where(part == 1, middle.astype(f32), jnp.where(part == 2, low.astype(f32), f32(0.0))),
    )

    def spot(xx, i):
        return pl.ds(pl.multiple_of((2 * i + xx) * block, block), block)

    def pair(i):
        return slice(2 * i * block, 2 * (i + 1) * block)

    xb[c, 0, spot(x, 0), :] = jnp.concatenate(
        [
            jnp.concatenate([tok[:, :half], coded], axis=1),
            jnp.concatenate([tok[:, half:], jnp.zeros_like(coded)], axis=1),
        ],
        axis=0,
    ).astype(bf16)

    pl.semaphore_wait(barrier, greeted)
    sends = []

    def go(copy):
        copy.start()
        sends.append(copy)

    z_copy = [None] + [
        remote(xb.at[c, 0, spot(x, 0), :], xb.at[c, 0, spot(x, i), :], z_sem, i, dev(x, y, along(i), c))
        for i in range(1, nz)
    ]
    x_copy = [remote(xb.at[c, 0, spot(x, i), :], xb.at[c, 0, spot(x, i), :], x_sem, i, x_peer) for i in range(nz)]
    x_land = [remote(xb.at[c, 0, spot(ox, i), :], xb.at[c, 0, spot(ox, i), :], x_sem, i, x_peer) for i in range(nz)]
    y_copy = [remote(xb.at[c, 0, spot(x, i), :], xb.at[c, 1, spot(x, i), :], y_sem, i, y_peer) for i in range(nz)]
    by_y = [i for i in range(nz) if i % 4 in (1, 2)]
    d_copy, d_land = [], []
    for i in range(nz):
        if i in by_y:
            d_copy.append(remote(xb.at[c, 0, spot(ox, i), :], xb.at[c, 1, spot(ox, i), :], dy_sem, i, y_peer))
            d_land.append(d_copy[-1])
        else:
            d_copy.append(remote(xb.at[c, 1, spot(x, i), :], xb.at[c, 1, spot(x, i), :], dx_sem, i, x_peer))
            d_land.append(remote(xb.at[c, 1, spot(ox, i), :], xb.at[c, 1, spot(ox, i), :], dx_sem, i, x_peer))
    sib_copy, sib_land = [
        [
            [remote(xb.at[k, s, pair(i), :], xb.at[k, s, pair(i), :], sib_sem, s * nz + i, sibling) for i in range(nz)]
            for s in range(2)
        ]
        for k in (c, oc)
    ]

    def assemble(s, i):
        sib_land[s][i].wait_recv()
        for b in (2 * i, 2 * i + 1):
            at = slice(b * block, (b + 1) * block)
            two = [xb[k, s, at, :].astype(f32) for k in range(2)]
            for h in range(2):
                lhs[s, h, at, :] = jnp.concatenate(
                    [v[h * rows : (h + 1) * rows, :half] for v in two], axis=0
                ).astype(bf16)
            tabs[s, at, :] = jnp.concatenate([v[:rows, half:] for v in two], axis=0)

    for i in range(1, nz):
        go(z_copy[i])
    go(x_copy[0])
    go(y_copy[0])
    for i in range(nz):
        if i + 1 < nz:
            z_copy[i + 1].wait_recv()
            go(x_copy[i + 1])
            go(y_copy[i + 1])
        x_land[i].wait_recv()
        if i in by_y:
            go(d_copy[i])
        go(sib_copy[0][i])
        y_copy[i].wait_recv()
        if i not in by_y:
            go(d_copy[i])
        if i:
            assemble(0, i - 1)
    assemble(0, nz - 1)

    def hid_copy(s, n):
        return remote(hid_out.at[s, n], hid_in.at[s, n], hid_sem, 2 * s + n, x_peer)

    def front(s):
        @pl.loop(0, 2)
        def _(n):
            cols = pl.ds(pl.multiple_of(n * ff_part, ff_part), ff_part)
            gate = dot32(lhs[s, 0], wg[0, :, cols]) + dot32(lhs[s, 1], wg[1, :, cols])
            up = dot32(lhs[s, 0], wu[0, :, cols]) + dot32(lhs[s, 1], wu[1, :, cols])
            hid_out[s, n] = (gate / (f32(1.0) + jnp.exp(-gate)) * up).astype(bf16)
            hid_copy(s, n).start()

    for load in loads[:4]:
        load.wait()
    front(0)
    for i in range(nz):
        d_land[i].wait_recv()
        go(sib_copy[1][i])
        if i:
            assemble(1, i - 1)
    assemble(1, nz - 1)
    front(1)

    for load in loads[4:]:
        load.wait()
    def part_copy(s, e):
        return remote(part_out.at[s, e], part_in.at[s, e], part_sem, 2 * s + e, sibling)

    lanes = lax.broadcasted_iota(jnp.int32, (stage, LANES), 1)
    wanted = (lanes % experts == 2 * p + y) & (lanes < 3 * experts)

    def ret_copy(s, e, i):
        to = dev(x, (oy if s else y), along(i), c)
        slot = (s * 2 + e) * nz + i
        return remote(ret_out.at[s, e, pair(i), :], ret_in.at[slot], ret_sem, slot, to)

    def back(s):
        weight = jnp.sum(jnp.where(wanted, tabs[s], f32(0.0)), axis=1, keepdims=True)
        for n in range(2):
            hid_copy(s, n).wait_recv()

        def piece_of(which, e):
            cols = pl.ds(pl.multiple_of(which * quarter + e * piece, piece), piece)
            total = jnp.zeros((stage, piece), f32)
            for n in range(2):
                span = slice(n * ff_part, (n + 1) * ff_part)
                total += dot32(hid_out[s, n], wd[0, span, cols]) + dot32(hid_in[s, n], wd[1, span, cols])
            return total * weight

        @pl.loop(0, 2)
        def _(e):
            part_out[s, e] = piece_of(oc, e).astype(bf16)
            part_copy(s, e).start()

        @pl.loop(0, 2)
        def _(e):
            own = piece_of(c, e)
            part_copy(s, e).wait_recv()
            ret_out[s, e] = (own + part_in[s, e].astype(f32)).astype(bf16)
            for i in reversed(range(nz)):
                if s or i:
                    ret_copy(s, e, i).start()

    back(0)
    back(1)

    for e in range(2):
        total = ret_out[0, e, pair(0), :].astype(f32)
        for s in range(2):
            for i in range(nz):
                if s or i:
                    ret_copy(s, e, i).wait_recv()
                    total += ret_in[(s * 2 + e) * nz + i].astype(f32)
        fin_out[:, e * piece : (e + 1) * piece] = total

    def rows_of(xx, cc):
        return pl.ds(pl.multiple_of((xx * 2 + cc) * rows, rows), rows)

    fin_copy = [
        remote(fin_out.at[rows_of(xx, cc), :], fin_in.at[n], fin_sem, n, to)
        for n, (xx, cc, to) in enumerate(((ox, c, x_peer), (ox, oc, x_sibling), (x, oc, sibling)))
    ]
    for copy in fin_copy:
        go(copy)
    kept = fin_out[rows_of(x, c), :]
    for copy in fin_copy:
        copy.wait_recv()
    pieces = []
    for h in range(2):
        for q in range(2):
            near = jnp.where(c == q, kept, fin_in[2])
            far = jnp.where(c == q, fin_in[0], fin_in[1])
            pieces.append(jnp.where(x == h, near, far))
    mixed = tok + jnp.concatenate(pieces, axis=1)
    factor = lax.rsqrt(jnp.mean(mixed * mixed, axis=1, keepdims=True) + 1e-06)
    out_ref[...] = (mixed * factor * gain_ref[...]).astype(bf16)
    for s in range(2):
        for e in range(2):
            hid_copy(s, e).wait_send()
            part_copy(s, e).wait_send()
            for i in range(nz):
                if s or i:
                    ret_copy(s, e, i).wait_send()
    for copy in sends:
        copy.wait_send()


def fused(tokens, expert_ids, gate_weights, w_gate, w_up, w_down, norm_gain):
    f32, bf16 = jnp.float32, jnp.bfloat16
    rows, width = tokens.shape
    n_ep = lax.axis_size("ep")
    nz, experts = n_ep // 2, 2 * n_ep
    half, quarter = width // 2, width // 4
    block = 2 * rows
    stage = 2 * nz * block
    wide = half + LANES
    ff_half, out_cols = w_gate.shape[2], w_down.shape[2]
    vmem = pltpu.VMEM

    def sems(count):
        return pltpu.SemaphoreType.DMA((2, count))

    return pl.pallas_call(
        functools.partial(fused_kernel, nz, experts),
        out_shape=jax.ShapeDtypeStruct((rows, width), bf16),
        in_specs=[pl.BlockSpec(memory_space=pltpu.HBM)] * 7,
        out_specs=pl.BlockSpec(memory_space=pltpu.VMEM),
        scratch_shapes=[
            vmem((rows, width), bf16),
            vmem(expert_ids.shape, jnp.int32),
            vmem(gate_weights.shape, f32),
            vmem((1, width), f32),
            vmem((2, half, ff_half), bf16),
            vmem((2, half, ff_half), bf16),
            vmem((2, ff_half, out_cols), bf16),
            vmem((2, 2, stage, wide), bf16),
            vmem((2, 2, stage, half), bf16),
            vmem((2, stage, LANES), f32),
            vmem((2, 2, stage, ff_half // 2), bf16),
            vmem((2, 2, stage, ff_half // 2), bf16),
            vmem((2, 2, stage, quarter // 2), bf16),
            vmem((2, 2, stage, quarter // 2), bf16),
            vmem((2, 2, stage, quarter // 2), bf16),
            vmem((4 * nz, 2 * block, quarter // 2), bf16),
            vmem((2 * block, quarter), f32),
            vmem((3, rows, quarter), f32),
            pltpu.SemaphoreType.DMA((4,)),
            pltpu.SemaphoreType.DMA((6,)),
            sems(nz), sems(nz), sems(nz), sems(nz), sems(nz), sems(2 * nz), sems(4), sems(4),
            sems(4 * nz), sems(3),
        ],
        compiler_params=pltpu.CompilerParams(
            collective_id=0, has_side_effects=True, vmem_limit_bytes=56 * 1024 * 1024
        ),
    )(tokens, expert_ids, gate_weights, norm_gain.reshape(1, width), w_gate, w_up, w_down)


def swapped(shard, axis, bit):
    return lax.ppermute(shard, axis, [(i, i ^ 1 << bit) for i in range(lax.axis_size(axis))])


def expert_front(arrived, gate_slice, up_slice):
    gate_part = jnp.einsum("abmd,df->abmf", arrived, gate_slice, preferred_element_type=jnp.float32)
    up_part = jnp.einsum("abmd,df->abmf", arrived, up_slice, preferred_element_type=jnp.float32)
    return (jax.nn.silu(gate_part) * up_part).astype(jnp.bfloat16)


def routed(tokens, expert_ids, gate_weights, w_gate, w_up, w_down, norm_gain):
    tok_rows, width = tokens.shape
    top_count = expert_ids.shape[1]
    n_ep = lax.axis_size("ep")
    n_grp = lax.axis_size("grp")
    experts = 2 * n_ep
    capacity = max(2, 2 * tok_rows * top_count // experts)
    slots = experts * capacity
    span = n_grp // 2
    flat_ids = expert_ids.reshape(-1)
    onehot = (flat_ids[:, None] == jnp.arange(experts, dtype=jnp.int32)[None, :]).astype(jnp.int32)
    earlier = jnp.cumsum(onehot, axis=0) - onehot
    ranking = jnp.sum(earlier * onehot, axis=1)
    slot_ids = jnp.arange(slots, dtype=jnp.int32)
    send_slot = flat_ids % 2 * (n_ep * capacity) + flat_ids // 2 * capacity + ranking
    placing = send_slot.reshape(tok_rows, top_count)[None, :, :] == slot_ids[:, None, None]
    placing = jnp.sum(placing.astype(jnp.float32), axis=2).astype(jnp.bfloat16)
    outgoing = jnp.dot(placing, tokens, preferred_element_type=jnp.float32).astype(jnp.bfloat16)
    outgoing = outgoing.reshape(2, n_ep, capacity, width)
    gate_slice = w_gate[0]
    up_slice = w_up[0]
    arrived = lax.all_to_all(outgoing, "ep", split_axis=1, concat_axis=1, tiled=True)
    fanned = jnp.repeat(arrived, span, axis=0)
    hidden = expert_front(
        lax.all_to_all(fanned, "grp", split_axis=0, concat_axis=0, tiled=True), gate_slice, up_slice
    )
    my_index = lax.axis_index("grp")
    assembled = hidden
    for level in range(span.bit_length() - 1):
        partner = swapped(assembled, "grp", level)
        upper = my_index // (1 << level) % 2
        assembled = jnp.where(
            upper == 0,
            jnp.concatenate([assembled, partner], axis=3),
            jnp.concatenate([partner, assembled], axis=3),
        )
    expert_out = jnp.einsum(
        "abmf,fc->abmc", assembled, w_down[0], preferred_element_type=jnp.float32
    ).astype(jnp.bfloat16)
    returned = lax.all_to_all(expert_out, "grp", split_axis=0, concat_axis=3, tiled=True)
    returned = returned.reshape(n_ep, capacity, 2, width)
    home = lax.all_to_all(returned, "ep", split_axis=0, concat_axis=0, tiled=True)
    back_slot = flat_ids // 2 * (capacity * 2) + ranking * 2 + flat_ids % 2
    matches = back_slot.reshape(tok_rows, top_count)[:, :, None] == slot_ids[None, None, :]
    weight_table = jnp.sum(jnp.where(matches, gate_weights[:, :, None], jnp.float32(0.0)), axis=1)
    combined = jnp.dot(
        weight_table,
        home.reshape(slots, width).astype(jnp.float32),
        precision=lax.Precision.HIGHEST,
    )
    mixed = tokens.astype(jnp.float32) + combined
    factor = lax.rsqrt(jnp.mean(mixed * mixed, axis=1, keepdims=True) + 1e-06)
    return (mixed * factor * norm_gain).astype(jnp.bfloat16)


def shards(tokens, *rest):
    all_rows = tokens.shape[0] * lax.axis_size("grp") * lax.axis_size("ep")
    dense = lax.axis_size("grp") == 4 and lax.axis_size("ep") == 8 and all_rows <= 256
    return (fused if dense else routed)(tokens, *rest)


def solution(mesh):
    placed = (
        P(("grp", "ep"), None),
        P(("grp", "ep"), None),
        P(("grp", "ep"), None),
        P("ep", None, "grp"),
        P("ep", None, "grp"),
        P("ep", None, "grp"),
        P(),
    )
    return jax.shard_map(
        shards, mesh=mesh, in_specs=placed, out_specs=P(("grp", "ep"), None), check_vma=False
    )
```

```python
import functools

import jax
import jax.numpy as jnp
from jax import lax
from jax.experimental import pallas as pl
from jax.experimental.pallas import tpu as pltpu
from jax.sharding import PartitionSpec as P

LANES = 128
MESH = pl.DeviceIdType.MESH


def dot32(a, b):
    return jnp.dot(a, b, preferred_element_type=jnp.float32)


def fused_kernel(
    nz, experts,
    tok_hbm, ids_hbm, gates_hbm, gain_hbm, wg_hbm, wu_hbm, wd_hbm, out_ref,
    tok_ref, ids_ref, gates_ref, gain_ref, wg, wu, wd, xb, lhs, tabs, hid_out, hid_in, part_out, part_in, ret_out, ret_in, fin_out, fin_in,
    t_sem, w_sem, z_sem, x_sem, y_sem, dx_sem, dy_sem, sib_sem, hid_sem, part_sem, ret_sem, fin_sem,
):
    f32, bf16 = jnp.float32, jnp.bfloat16
    rows, width = tok_ref.shape
    half = width // 2
    quarter = width // 4
    block = 2 * rows
    stage = 2 * nz * block
    piece = quarter // 2
    ff_half = wg.shape[2]
    ff_part = ff_half // 2
    g, p = lax.axis_index("grp"), lax.axis_index("ep")
    y, x = g // 2, g % 2
    z, c = p // 2, p % 2
    ox, oy, oc = 1 - x, 1 - y, 1 - c

    def dev(xx, yy, zz, cc):
        return (yy * 2 + xx, zz * 2 + cc)

    def along(i):
        return (z // 2 * 2 + (z + i) % 2 + i // 2 * 2) % nz

    def remote(src, dst, sems, idx, to):
        return pltpu.make_async_remote_copy(
            src_ref=src, dst_ref=dst, send_sem=sems.at[0, idx], recv_sem=sems.at[1, idx],
            device_id=to, device_id_type=MESH,
        )

    sibling = dev(x, y, z, oc)
    x_peer = dev(ox, y, z, c)
    y_peer = dev(x, oy, z, c)
    x_sibling = dev(ox, y, z, oc)

    small = [
        pltpu.make_async_copy(src, dst, t_sem.at[n])
        for n, (src, dst) in enumerate(
            ((tok_hbm, tok_ref), (ids_hbm, ids_ref), (gates_hbm, gates_ref), (gain_hbm, gain_ref))
        )
    ]
    for load in small:
        load.start()

    loads = []
    n = 0
    for k in range(2):
        for src, dst in ((wg_hbm, wg), (wu_hbm, wu)):
            loads.append(pltpu.make_async_copy(src.at[0, pl.ds(k * half, half), :], dst.at[k], w_sem.at[n]))
            n += 1
    for mine, at_k in ((0, x), (1, ox)):
        span = pl.ds(pl.multiple_of(at_k * ff_half, ff_half), ff_half)
        loads.append(pltpu.make_async_copy(wd_hbm.at[0, span, :], wd.at[mine], w_sem.at[n]))
        n += 1

    barrier = pltpu.get_barrier_semaphore()
    greeted = 0
    for to in [dev(x, (y + dy) % 2, (z + dz) % nz, c) for dy in range(2) for dz in range(nz) if dy or dz] + [
        x_peer, sibling, x_sibling
    ]:
        pl.semaphore_signal(barrier, inc=1, device_id=to, device_id_type=MESH)
        greeted += 1
    for load in small:
        load.wait()
    for load in loads:
        load.start()

    lane = lax.broadcasted_iota(jnp.int32, (rows, LANES), 1)
    table = jnp.zeros((rows, LANES), f32)
    for k in range(ids_ref.shape[1]):
        table += jnp.where(ids_ref[:, k : k + 1] == lane % experts, gates_ref[:, k : k + 1], f32(0.0))
    tok = tok_ref[...].astype(f32)
    high = table.astype(bf16)
    rest = table - high.astype(f32)
    middle = rest.astype(bf16)
    low = (rest - middle.astype(f32)).astype(bf16)
    part = lane // experts
    coded = jnp.where(
        part == 0, high.astype(f32),
        jnp.where(part == 1, middle.astype(f32), jnp.where(part == 2, low.astype(f32), f32(0.0))),
    )

    def spot(xx, i):
        return pl.ds(pl.multiple_of((2 * i + xx) * block, block), block)

    def pair(i):
        return slice(2 * i * block, 2 * (i + 1) * block)

    xb[c, 0, spot(x, 0), :] = jnp.concatenate(
        [
            jnp.concatenate([tok[:, :half], coded], axis=1),
            jnp.concatenate([tok[:, half:], jnp.zeros_like(coded)], axis=1),
        ],
        axis=0,
    ).astype(bf16)

    pl.semaphore_wait(barrier, greeted)
    sends = []

    def go(copy):
        copy.start()
        sends.append(copy)

    z_copy = [None] + [
        remote(xb.at[c, 0, spot(x, 0), :], xb.at[c, 0, spot(x, i), :], z_sem, i, dev(x, y, along(i), c))
        for i in range(1, nz)
    ]
    x_copy = [remote(xb.at[c, 0, spot(x, i), :], xb.at[c, 0, spot(x, i), :], x_sem, i, x_peer) for i in range(nz)]
    x_land = [remote(xb.at[c, 0, spot(ox, i), :], xb.at[c, 0, spot(ox, i), :], x_sem, i, x_peer) for i in range(nz)]
    y_copy = [remote(xb.at[c, 0, spot(x, i), :], xb.at[c, 1, spot(x, i), :], y_sem, i, y_peer) for i in range(nz)]
    by_y = [i for i in range(nz) if i % 4 in (1, 2)]
    d_copy, d_land = [], []
    for i in range(nz):
        if i in by_y:
            d_copy.append(remote(xb.at[c, 0, spot(ox, i), :], xb.at[c, 1, spot(ox, i), :], dy_sem, i, y_peer))
            d_land.append(d_copy[-1])
        else:
            d_copy.append(remote(xb.at[c, 1, spot(x, i), :], xb.at[c, 1, spot(x, i), :], dx_sem, i, x_peer))
            d_land.append(remote(xb.at[c, 1, spot(ox, i), :], xb.at[c, 1, spot(ox, i), :], dx_sem, i, x_peer))
    sib_copy, sib_land = [
        [
            [remote(xb.at[k, s, pair(i), :], xb.at[k, s, pair(i), :], sib_sem, s * nz + i, sibling) for i in range(nz)]
            for s in range(2)
        ]
        for k in (c, oc)
    ]

    def assemble(s, i):
        sib_land[s][i].wait_recv()
        for b in (2 * i, 2 * i + 1):
            at = slice(b * block, (b + 1) * block)
            two = [xb[k, s, at, :].astype(f32) for k in range(2)]
            for h in range(2):
                lhs[s, h, at, :] = jnp.concatenate(
                    [v[h * rows : (h + 1) * rows, :half] for v in two], axis=0
                ).astype(bf16)
            tabs[s, at, :] = jnp.concatenate([v[:rows, half:] for v in two], axis=0)

    for i in range(1, nz):
        go(z_copy[i])
    go(x_copy[0])
    go(y_copy[0])
    def onward(i):
        z_copy[i].wait_recv()
        go(x_copy[i])
        go(y_copy[i])

    def arrive(i):
        x_land[i].wait_recv()
        if i in by_y:
            go(d_copy[i])
        go(sib_copy[0][i])
        y_copy[i].wait_recv()
        if i not in by_y:
            go(d_copy[i])

    def arrive_far(i):
        d_land[i].wait_recv()
        go(sib_copy[1][i])

    mid = nz // 2
    chunks = [(0, 0, range(0, mid)), (1, 0, range(mid, nz)), (2, 1, range(0, mid)), (3, 1, range(mid, nz))]

    def rows_in(pairs):
        return slice(2 * pairs[0] * block, 2 * (pairs[-1] + 1) * block)

    def hid_copy(chunk, n):
        number, s, pairs = chunk
        at = rows_in(pairs)
        return remote(hid_out.at[s, n, at], hid_in.at[s, n, at], hid_sem, 2 * number + n, x_peer)

    def front(chunk):
        number, s, pairs = chunk
        at = rows_in(pairs)
        for i in pairs:
            assemble(s, i)
        if number == 0:
            for load in loads[:4]:
                load.wait()

        @pl.loop(0, 2)
        def _(n):
            cols = pl.ds(pl.multiple_of(n * ff_part, ff_part), ff_part)
            gate = dot32(lhs[s, 0, at], wg[0, :, cols]) + dot32(lhs[s, 1, at], wg[1, :, cols])
            up = dot32(lhs[s, 0, at], wu[0, :, cols]) + dot32(lhs[s, 1, at], wu[1, :, cols])
            hid_out[s, n, at] = (gate / (f32(1.0) + jnp.exp(-gate)) * up).astype(bf16)
            hid_copy(chunk, n).start()

    def part_copy(chunk, e):
        number, s, pairs = chunk
        at = rows_in(pairs)
        return remote(part_out.at[s, e, at], part_in.at[s, e, at], part_sem, 2 * number + e, sibling)

    lanes = lax.broadcasted_iota(jnp.int32, (stage // 2, LANES), 1)
    wanted = (lanes % experts == 2 * p + y) & (lanes < 3 * experts)

    def ret_copy(s, e, i):
        to = dev(x, (oy if s else y), along(i), c)
        slot = (s * 2 + e) * nz + i
        return remote(ret_out.at[s, e, pair(i), :], ret_in.at[slot], ret_sem, slot, to)

    def piece_of(chunk, which, e):
        number, s, pairs = chunk
        at = rows_in(pairs)
        cols = pl.ds(pl.multiple_of(which * quarter + e * piece, piece), piece)
        total = jnp.zeros((len(pairs) * 2 * block, piece), f32)
        for n in range(2):
            span = slice(n * ff_part, (n + 1) * ff_part)
            total += dot32(hid_out[s, n, at], wd[0, span, cols]) + dot32(hid_in[s, n, at], wd[1, span, cols])
        weight = jnp.sum(jnp.where(wanted, tabs[s, at], f32(0.0)), axis=1, keepdims=True)
        return total * weight

    def back_theirs(chunk):
        number, s, pairs = chunk
        at = rows_in(pairs)
        if number == 0:
            for load in loads[4:]:
                load.wait()
        for n in range(2):
            hid_copy(chunk, n).wait_recv()

        @pl.loop(0, 2)
        def _(e):
            part_out[s, e, at] = piece_of(chunk, oc, e).astype(bf16)
            part_copy(chunk, e).start()

    def back_mine(chunk):
        number, s, pairs = chunk
        at = rows_in(pairs)

        @pl.loop(0, 2)
        def _(e):
            own = piece_of(chunk, c, e)
            part_copy(chunk, e).wait_recv()
            ret_out[s, e, at] = (own + part_in[s, e, at].astype(f32)).astype(bf16)
            for i in reversed(pairs):
                if s or i:
                    ret_copy(s, e, i).start()

    onward(1)
    arrive(0)
    for i in range(2, nz):
        onward(i)
    for i in range(1, mid):
        arrive(i)
    front(chunks[0])
    for i in range(mid):
        arrive_far(i)
    for i in range(mid, nz):
        arrive(i)
    front(chunks[1])
    for i in range(mid, nz):
        arrive_far(i)
    front(chunks[2])
    back_theirs(chunks[0])
    front(chunks[3])
    back_mine(chunks[0])
    back_theirs(chunks[1])
    back_theirs(chunks[2])
    back_mine(chunks[1])
    back_mine(chunks[2])
    back_theirs(chunks[3])
    back_mine(chunks[3])

    for e in range(2):
        total = ret_out[0, e, pair(0), :].astype(f32)
        for s in range(2):
            for i in range(nz):
                if s or i:
                    ret_copy(s, e, i).wait_recv()
                    total += ret_in[(s * 2 + e) * nz + i].astype(f32)
        fin_out[:, e * piece : (e + 1) * piece] = total

    def rows_of(xx, cc):
        return pl.ds(pl.multiple_of((xx * 2 + cc) * rows, rows), rows)

    fin_copy = [
        remote(fin_out.at[rows_of(xx, cc), :], fin_in.at[n], fin_sem, n, to)
        for n, (xx, cc, to) in enumerate(((ox, c, x_peer), (ox, oc, x_sibling), (x, oc, sibling)))
    ]
    for copy in fin_copy:
        go(copy)
    kept = fin_out[rows_of(x, c), :]
    for copy in fin_copy:
        copy.wait_recv()
    pieces = []
    for h in range(2):
        for q in range(2):
            near = jnp.where(c == q, kept, fin_in[2])
            far = jnp.where(c == q, fin_in[0], fin_in[1])
            pieces.append(jnp.where(x == h, near, far))
    mixed = tok + jnp.concatenate(pieces, axis=1)
    factor = lax.rsqrt(jnp.mean(mixed * mixed, axis=1, keepdims=True) + 1e-06)
    out_ref[...] = (mixed * factor * gain_ref[...]).astype(bf16)
    for chunk in chunks:
        s, pairs = chunk[1:]
        for e in range(2):
            hid_copy(chunk, e).wait_send()
            part_copy(chunk, e).wait_send()
            for i in pairs:
                if s or i:
                    ret_copy(s, e, i).wait_send()
    for copy in sends:
        copy.wait_send()


def fused(tokens, expert_ids, gate_weights, w_gate, w_up, w_down, norm_gain):
    f32, bf16 = jnp.float32, jnp.bfloat16
    rows, width = tokens.shape
    n_ep = lax.axis_size("ep")
    nz, experts = n_ep // 2, 2 * n_ep
    half, quarter = width // 2, width // 4
    block = 2 * rows
    stage = 2 * nz * block
    wide = half + LANES
    ff_half, out_cols = w_gate.shape[2], w_down.shape[2]
    vmem = pltpu.VMEM

    def sems(count):
        return pltpu.SemaphoreType.DMA((2, count))

    return pl.pallas_call(
        functools.partial(fused_kernel, nz, experts),
        out_shape=jax.ShapeDtypeStruct((rows, width), bf16),
        in_specs=[pl.BlockSpec(memory_space=pltpu.HBM)] * 7,
        out_specs=pl.BlockSpec(memory_space=pltpu.VMEM),
        scratch_shapes=[
            vmem((rows, width), bf16),
            vmem(expert_ids.shape, jnp.int32),
            vmem(gate_weights.shape, f32),
            vmem((1, width), f32),
            vmem((2, half, ff_half), bf16),
            vmem((2, half, ff_half), bf16),
            vmem((2, ff_half, out_cols), bf16),
            vmem((2, 2, stage, wide), bf16),
            vmem((2, 2, stage, half), bf16),
            vmem((2, stage, LANES), f32),
            vmem((2, 2, stage, ff_half // 2), bf16),
            vmem((2, 2, stage, ff_half // 2), bf16),
            vmem((2, 2, stage, quarter // 2), bf16),
            vmem((2, 2, stage, quarter // 2), bf16),
            vmem((2, 2, stage, quarter // 2), bf16),
            vmem((4 * nz, 2 * block, quarter // 2), bf16),
            vmem((2 * block, quarter), f32),
            vmem((3, rows, quarter), f32),
            pltpu.SemaphoreType.DMA((4,)),
            pltpu.SemaphoreType.DMA((6,)),
            sems(nz), sems(nz), sems(nz), sems(nz), sems(nz), sems(2 * nz), sems(8), sems(8),
            sems(4 * nz), sems(3),
        ],
        compiler_params=pltpu.CompilerParams(
            collective_id=0, has_side_effects=True, vmem_limit_bytes=56 * 1024 * 1024
        ),
    )(tokens, expert_ids, gate_weights, norm_gain.reshape(1, width), w_gate, w_up, w_down)


def swapped(shard, axis, bit):
    return lax.ppermute(shard, axis, [(i, i ^ 1 << bit) for i in range(lax.axis_size(axis))])


def expert_front(arrived, gate_slice, up_slice):
    gate_part = jnp.einsum("abmd,df->abmf", arrived, gate_slice, preferred_element_type=jnp.float32)
    up_part = jnp.einsum("abmd,df->abmf", arrived, up_slice, preferred_element_type=jnp.float32)
    return (jax.nn.silu(gate_part) * up_part).astype(jnp.bfloat16)


def routed(tokens, expert_ids, gate_weights, w_gate, w_up, w_down, norm_gain):
    tok_rows, width = tokens.shape
    top_count = expert_ids.shape[1]
    n_ep = lax.axis_size("ep")
    n_grp = lax.axis_size("grp")
    experts = 2 * n_ep
    capacity = max(2, 2 * tok_rows * top_count // experts)
    slots = experts * capacity
    span = n_grp // 2
    flat_ids = expert_ids.reshape(-1)
    onehot = (flat_ids[:, None] == jnp.arange(experts, dtype=jnp.int32)[None, :]).astype(jnp.int32)
    earlier = jnp.cumsum(onehot, axis=0) - onehot
    ranking = jnp.sum(earlier * onehot, axis=1)
    slot_ids = jnp.arange(slots, dtype=jnp.int32)
    send_slot = flat_ids % 2 * (n_ep * capacity) + flat_ids // 2 * capacity + ranking
    placing = send_slot.reshape(tok_rows, top_count)[None, :, :] == slot_ids[:, None, None]
    placing = jnp.sum(placing.astype(jnp.float32), axis=2).astype(jnp.bfloat16)
    outgoing = jnp.dot(placing, tokens, preferred_element_type=jnp.float32).astype(jnp.bfloat16)
    outgoing = outgoing.reshape(2, n_ep, capacity, width)
    gate_slice = w_gate[0]
    up_slice = w_up[0]
    arrived = lax.all_to_all(outgoing, "ep", split_axis=1, concat_axis=1, tiled=True)
    fanned = jnp.repeat(arrived, span, axis=0)
    hidden = expert_front(
        lax.all_to_all(fanned, "grp", split_axis=0, concat_axis=0, tiled=True), gate_slice, up_slice
    )
    my_index = lax.axis_index("grp")
    assembled = hidden
    for level in range(span.bit_length() - 1):
        partner = swapped(assembled, "grp", level)
        upper = my_index // (1 << level) % 2
        assembled = jnp.where(
            upper == 0,
            jnp.concatenate([assembled, partner], axis=3),
            jnp.concatenate([partner, assembled], axis=3),
        )
    expert_out = jnp.einsum(
        "abmf,fc->abmc", assembled, w_down[0], preferred_element_type=jnp.float32
    ).astype(jnp.bfloat16)
    returned = lax.all_to_all(expert_out, "grp", split_axis=0, concat_axis=3, tiled=True)
    returned = returned.reshape(n_ep, capacity, 2, width)
    home = lax.all_to_all(returned, "ep", split_axis=0, concat_axis=0, tiled=True)
    back_slot = flat_ids // 2 * (capacity * 2) + ranking * 2 + flat_ids % 2
    matches = back_slot.reshape(tok_rows, top_count)[:, :, None] == slot_ids[None, None, :]
    weight_table = jnp.sum(jnp.where(matches, gate_weights[:, :, None], jnp.float32(0.0)), axis=1)
    combined = jnp.dot(
        weight_table,
        home.reshape(slots, width).astype(jnp.float32),
        precision=lax.Precision.HIGHEST,
    )
    mixed = tokens.astype(jnp.float32) + combined
    factor = lax.rsqrt(jnp.mean(mixed * mixed, axis=1, keepdims=True) + 1e-06)
    return (mixed * factor * norm_gain).astype(jnp.bfloat16)


def shards(tokens, *rest):
    all_rows = tokens.shape[0] * lax.axis_size("grp") * lax.axis_size("ep")
    dense = lax.axis_size("grp") == 4 and lax.axis_size("ep") == 8 and all_rows <= 256
    return (fused if dense else routed)(tokens, *rest)


def solution(mesh):
    placed = (
        P(("grp", "ep"), None),
        P(("grp", "ep"), None),
        P(("grp", "ep"), None),
        P("ep", None, "grp"),
        P("ep", None, "grp"),
        P("ep", None, "grp"),
        P(),
    )
    return jax.shard_map(
        shards, mesh=mesh, in_specs=placed, out_specs=P(("grp", "ep"), None), check_vma=False
    )
```

```python
import functools

import jax
import jax.numpy as jnp
from jax import lax
from jax.experimental import pallas as pl
from jax.experimental.pallas import tpu as pltpu
from jax.sharding import PartitionSpec as P

LANES = 128
MESH = pl.DeviceIdType.MESH


def dot32(a, b):
    return jnp.dot(a, b, preferred_element_type=jnp.float32)


def fused_kernel(
    nz, experts,
    tok_hbm, ids_hbm, gates_hbm, gain_hbm, wg_hbm, wu_hbm, wd_hbm, out_ref,
    tok_ref, ids_ref, gates_ref, gain_ref, wgu, wd, xb, lhs, tabs, hid, part_out, part_in, ret_out, ret_in, fin_out, fin_in,
    t_sem, w_sem, z_sem, x_sem, y_sem, dx_sem, dy_sem, sib_sem, hid_sem, part_sem, ret_sem, fin_sem,
):
    f32, bf16 = jnp.float32, jnp.bfloat16
    rows, width = tok_ref.shape
    half = width // 2
    quarter = width // 4
    block = 2 * rows
    stage = 2 * nz * block
    piece = quarter // 2
    ff_part = wgu.shape[2] // 2
    ff_half = 2 * ff_part
    g, p = lax.axis_index("grp"), lax.axis_index("ep")
    y, x = g // 2, g % 2
    z, c = p // 2, p % 2
    ox, oy, oc = 1 - x, 1 - y, 1 - c

    def dev(xx, yy, zz, cc):
        return (yy * 2 + xx, zz * 2 + cc)

    def along(i):
        return (z // 2 * 2 + (z + i) % 2 + i // 2 * 2) % nz

    def remote(src, dst, sems, idx, to):
        return pltpu.make_async_remote_copy(
            src_ref=src, dst_ref=dst, send_sem=sems.at[0, idx], recv_sem=sems.at[1, idx],
            device_id=to, device_id_type=MESH,
        )

    sibling = dev(x, y, z, oc)
    x_peer = dev(ox, y, z, c)
    y_peer = dev(x, oy, z, c)
    x_sibling = dev(ox, y, z, oc)

    small = [
        pltpu.make_async_copy(src, dst, t_sem.at[n])
        for n, (src, dst) in enumerate(
            ((tok_hbm, tok_ref), (ids_hbm, ids_ref), (gates_hbm, gates_ref), (gain_hbm, gain_ref))
        )
    ]
    for load in small:
        load.start()

    loads = []
    for n in range(2):
        for k, src in enumerate((wg_hbm, wu_hbm)):
            from_cols, to_cols = pl.ds(n * ff_part, ff_part), pl.ds(k * ff_part, ff_part)
            loads.append(
                pltpu.make_async_copy(src.at[0, :, from_cols], wgu.at[n, :, to_cols], w_sem.at[len(loads)])
            )
    for mine, at_k in ((0, x), (1, ox)):
        span = pl.ds(pl.multiple_of(at_k * ff_half, ff_half), ff_half)
        for e in range(4):
            loads.append(
                pltpu.make_async_copy(
                    wd_hbm.at[0, span, pl.ds(e * piece, piece)],
                    wd.at[e, pl.ds(mine * ff_half, ff_half), :],
                    w_sem.at[len(loads)],
                )
            )

    barrier = pltpu.get_barrier_semaphore()
    greeted = 0
    for to in [dev(x, (y + dy) % 2, (z + dz) % nz, c) for dy in range(2) for dz in range(nz) if dy or dz] + [
        x_peer, sibling, x_sibling
    ]:
        pl.semaphore_signal(barrier, inc=1, device_id=to, device_id_type=MESH)
        greeted += 1
    for load in small:
        load.wait()
    for load in loads:
        load.start()

    lane = lax.broadcasted_iota(jnp.int32, (rows, LANES), 1)
    table = jnp.zeros((rows, LANES), f32)
    for k in range(ids_ref.shape[1]):
        table += jnp.where(ids_ref[:, k : k + 1] == lane % experts, gates_ref[:, k : k + 1], f32(0.0))
    tok = tok_ref[...].astype(f32)
    high = table.astype(bf16)
    rest = table - high.astype(f32)
    middle = rest.astype(bf16)
    low = (rest - middle.astype(f32)).astype(bf16)
    part = lane // experts
    coded = jnp.where(
        part == 0, high.astype(f32),
        jnp.where(part == 1, middle.astype(f32), jnp.where(part == 2, low.astype(f32), f32(0.0))),
    )

    def spot(xx, i):
        return pl.ds(pl.multiple_of((2 * i + xx) * block, block), block)

    def pair(i):
        return slice(2 * i * block, 2 * (i + 1) * block)

    xb[c, 0, spot(x, 0), :] = jnp.concatenate(
        [
            jnp.concatenate([tok[:, :half], coded], axis=1),
            jnp.concatenate([tok[:, half:], jnp.zeros_like(coded)], axis=1),
        ],
        axis=0,
    ).astype(bf16)

    pl.semaphore_wait(barrier, greeted)
    sends = []

    def go(copy):
        copy.start()
        sends.append(copy)

    z_copy = [None] + [
        remote(xb.at[c, 0, spot(x, 0), :], xb.at[c, 0, spot(x, i), :], z_sem, i, dev(x, y, along(i), c))
        for i in range(1, nz)
    ]
    x_copy = [remote(xb.at[c, 0, spot(x, i), :], xb.at[c, 0, spot(x, i), :], x_sem, i, x_peer) for i in range(nz)]
    x_land = [remote(xb.at[c, 0, spot(ox, i), :], xb.at[c, 0, spot(ox, i), :], x_sem, i, x_peer) for i in range(nz)]
    y_copy = [remote(xb.at[c, 0, spot(x, i), :], xb.at[c, 1, spot(x, i), :], y_sem, i, y_peer) for i in range(nz)]
    by_y = [i for i in range(nz) if i % 4 in (1, 2)]
    d_copy, d_land = [], []
    for i in range(nz):
        if i in by_y:
            d_copy.append(remote(xb.at[c, 0, spot(ox, i), :], xb.at[c, 1, spot(ox, i), :], dy_sem, i, y_peer))
            d_land.append(d_copy[-1])
        else:
            d_copy.append(remote(xb.at[c, 1, spot(x, i), :], xb.at[c, 1, spot(x, i), :], dx_sem, i, x_peer))
            d_land.append(remote(xb.at[c, 1, spot(ox, i), :], xb.at[c, 1, spot(ox, i), :], dx_sem, i, x_peer))
    sib_copy, sib_land = [
        [
            [remote(xb.at[k, s, pair(i), :], xb.at[k, s, pair(i), :], sib_sem, s * nz + i, sibling) for i in range(nz)]
            for s in range(2)
        ]
        for k in (c, oc)
    ]

    def assemble(s, i):
        sib_land[s][i].wait_recv()
        for b in (2 * i, 2 * i + 1):
            at = slice(b * block, (b + 1) * block)
            two = [xb[k, s, at, :].astype(f32) for k in range(2)]
            for h in range(2):
                lhs[s, at, h * half : (h + 1) * half] = jnp.concatenate(
                    [v[h * rows : (h + 1) * rows, :half] for v in two], axis=0
                ).astype(bf16)
            tabs[s, at, :] = jnp.concatenate([v[:rows, half:] for v in two], axis=0)

    for i in range(1, nz):
        go(z_copy[i])
    go(x_copy[0])
    go(y_copy[0])
    def onward(i):
        z_copy[i].wait_recv()
        go(x_copy[i])
        go(y_copy[i])

    def arrive(i):
        x_land[i].wait_recv()
        if i in by_y:
            go(d_copy[i])
        go(sib_copy[0][i])
        y_copy[i].wait_recv()
        if i not in by_y:
            go(d_copy[i])

    def arrive_far(i):
        d_land[i].wait_recv()
        go(sib_copy[1][i])

    chunks = [(0, 0, range(nz)), (1, 1, range(nz))]

    def rows_in(pairs):
        return slice(2 * pairs[0] * block, 2 * (pairs[-1] + 1) * block)

    def hid_copy(chunk, n):
        number, s, pairs = chunk
        at = rows_in(pairs)
        return remote(hid.at[s, n, at], hid.at[s, 2 + n, at], hid_sem, 2 * number + n, x_peer)

    def front(chunk):
        number, s, pairs = chunk
        at = rows_in(pairs)
        assemble(s, pairs[-1])
        if number == 0:
            for load in loads[:4]:
                load.wait()

        @pl.loop(0, 2)
        def _(n):
            both = dot32(lhs[s, at], wgu[n])
            gate, up = both[:, :ff_part], both[:, ff_part:]
            hid[s, n, at] = (gate / (f32(1.0) + jnp.exp(-gate)) * up).astype(bf16)
            hid_copy(chunk, n).start()

    def part_copy(chunk, e):
        number, s, pairs = chunk
        at = rows_in(pairs)
        return remote(part_out.at[s, e, at], part_in.at[s, e, at], part_sem, 2 * number + e, sibling)

    lanes = lax.broadcasted_iota(jnp.int32, (stage, LANES), 1)
    wanted = (lanes % experts == 2 * p + y) & (lanes < 3 * experts)

    def ret_copy(s, e, i):
        to = dev(x, (oy if s else y), along(i), c)
        slot = (s * 2 + e) * nz + i
        return remote(ret_out.at[s, e, pair(i), :], ret_in.at[slot], ret_sem, slot, to)

    def piece_of(chunk, which, e):
        number, s, pairs = chunk
        at = rows_in(pairs)
        total = dot32(jnp.concatenate([hid[s, n, at] for n in range(4)], axis=1), wd[which * 2 + e])
        weight = jnp.sum(jnp.where(wanted, tabs[s, at], f32(0.0)), axis=1, keepdims=True)
        return total * weight

    def back_theirs(chunk):
        number, s, pairs = chunk
        at = rows_in(pairs)
        if number == 0:
            for load in loads[4:]:
                load.wait()
        for n in range(2):
            hid_copy(chunk, n).wait_recv()

        @pl.loop(0, 2)
        def _(e):
            part_out[s, e, at] = piece_of(chunk, oc, e).astype(bf16)
            part_copy(chunk, e).start()

    def back_mine(chunk):
        number, s, pairs = chunk
        at = rows_in(pairs)

        @pl.loop(0, 2)
        def _(e):
            own = piece_of(chunk, c, e)
            part_copy(chunk, e).wait_recv()
            ret_out[s, e, at] = (own + part_in[s, e, at].astype(f32)).astype(bf16)
            for i in reversed(pairs):
                if s or i:
                    ret_copy(s, e, i).start()

    for i in range(nz):
        if i + 1 < nz:
            onward(i + 1)
        arrive(i)
        if i:
            assemble(0, i - 1)
    front(chunks[0])
    for i in range(nz):
        arrive_far(i)
        if i:
            assemble(1, i - 1)
    front(chunks[1])
    for chunk in chunks:
        back_theirs(chunk)
        back_mine(chunk)

    for e in range(2):
        total = ret_out[0, e, pair(0), :].astype(f32)
        for s in range(2):
            for i in range(nz):
                if s or i:
                    ret_copy(s, e, i).wait_recv()
                    total += ret_in[(s * 2 + e) * nz + i].astype(f32)
        fin_out[:, e * piece : (e + 1) * piece] = total

    def rows_of(xx, cc):
        return pl.ds(pl.multiple_of((xx * 2 + cc) * rows, rows), rows)

    fin_copy = [
        remote(fin_out.at[rows_of(xx, cc), :], fin_in.at[n], fin_sem, n, to)
        for n, (xx, cc, to) in enumerate(((ox, c, x_peer), (ox, oc, x_sibling), (x, oc, sibling)))
    ]
    for copy in fin_copy:
        go(copy)
    kept = fin_out[rows_of(x, c), :]
    for copy in fin_copy:
        copy.wait_recv()
    pieces = []
    for h in range(2):
        for q in range(2):
            near = jnp.where(c == q, kept, fin_in[2])
            far = jnp.where(c == q, fin_in[0], fin_in[1])
            pieces.append(jnp.where(x == h, near, far))
    mixed = tok + jnp.concatenate(pieces, axis=1)
    factor = lax.rsqrt(jnp.mean(mixed * mixed, axis=1, keepdims=True) + 1e-06)
    out_ref[...] = (mixed * factor * gain_ref[...]).astype(bf16)
    for chunk in chunks:
        s, pairs = chunk[1:]
        for e in range(2):
            hid_copy(chunk, e).wait_send()
            part_copy(chunk, e).wait_send()
            for i in pairs:
                if s or i:
                    ret_copy(s, e, i).wait_send()
    for copy in sends:
        copy.wait_send()


def fused(tokens, expert_ids, gate_weights, w_gate, w_up, w_down, norm_gain):
    f32, bf16 = jnp.float32, jnp.bfloat16
    rows, width = tokens.shape
    n_ep = lax.axis_size("ep")
    nz, experts = n_ep // 2, 2 * n_ep
    half, quarter = width // 2, width // 4
    block = 2 * rows
    stage = 2 * nz * block
    wide = half + LANES
    ff_half = w_gate.shape[2]
    vmem = pltpu.VMEM

    def sems(count):
        return pltpu.SemaphoreType.DMA((2, count))

    return pl.pallas_call(
        functools.partial(fused_kernel, nz, experts),
        out_shape=jax.ShapeDtypeStruct((rows, width), bf16),
        in_specs=[pl.BlockSpec(memory_space=pltpu.HBM)] * 7,
        out_specs=pl.BlockSpec(memory_space=pltpu.VMEM),
        scratch_shapes=[
            vmem((rows, width), bf16),
            vmem(expert_ids.shape, jnp.int32),
            vmem(gate_weights.shape, f32),
            vmem((1, width), f32),
            vmem((2, width, ff_half), bf16),
            vmem((4, 2 * ff_half, quarter // 2), bf16),
            vmem((2, 2, stage, wide), bf16),
            vmem((2, stage, width), bf16),
            vmem((2, stage, LANES), f32),
            vmem((2, 4, stage, ff_half // 2), bf16),
            vmem((2, 2, stage, quarter // 2), bf16),
            vmem((2, 2, stage, quarter // 2), bf16),
            vmem((2, 2, stage, quarter // 2), bf16),
            vmem((4 * nz, 2 * block, quarter // 2), bf16),
            vmem((2 * block, quarter), f32),
            vmem((3, rows, quarter), f32),
            pltpu.SemaphoreType.DMA((4,)),
            pltpu.SemaphoreType.DMA((12,)),
            sems(nz), sems(nz), sems(nz), sems(nz), sems(nz), sems(2 * nz), sems(4), sems(4),
            sems(4 * nz), sems(3),
        ],
        compiler_params=pltpu.CompilerParams(
            collective_id=0, has_side_effects=True, vmem_limit_bytes=56 * 1024 * 1024
        ),
    )(tokens, expert_ids, gate_weights, norm_gain.reshape(1, width), w_gate, w_up, w_down)


def swapped(shard, axis, bit):
    return lax.ppermute(shard, axis, [(i, i ^ 1 << bit) for i in range(lax.axis_size(axis))])


def expert_front(arrived, gate_slice, up_slice):
    gate_part = jnp.einsum("abmd,df->abmf", arrived, gate_slice, preferred_element_type=jnp.float32)
    up_part = jnp.einsum("abmd,df->abmf", arrived, up_slice, preferred_element_type=jnp.float32)
    return (jax.nn.silu(gate_part) * up_part).astype(jnp.bfloat16)


def routed(tokens, expert_ids, gate_weights, w_gate, w_up, w_down, norm_gain):
    tok_rows, width = tokens.shape
    top_count = expert_ids.shape[1]
    n_ep = lax.axis_size("ep")
    n_grp = lax.axis_size("grp")
    experts = 2 * n_ep
    capacity = max(2, 2 * tok_rows * top_count // experts)
    slots = experts * capacity
    span = n_grp // 2
    flat_ids = expert_ids.reshape(-1)
    onehot = (flat_ids[:, None] == jnp.arange(experts, dtype=jnp.int32)[None, :]).astype(jnp.int32)
    earlier = jnp.cumsum(onehot, axis=0) - onehot
    ranking = jnp.sum(earlier * onehot, axis=1)
    slot_ids = jnp.arange(slots, dtype=jnp.int32)
    send_slot = flat_ids % 2 * (n_ep * capacity) + flat_ids // 2 * capacity + ranking
    placing = send_slot.reshape(tok_rows, top_count)[None, :, :] == slot_ids[:, None, None]
    placing = jnp.sum(placing.astype(jnp.float32), axis=2).astype(jnp.bfloat16)
    outgoing = jnp.dot(placing, tokens, preferred_element_type=jnp.float32).astype(jnp.bfloat16)
    outgoing = outgoing.reshape(2, n_ep, capacity, width)
    gate_slice = w_gate[0]
    up_slice = w_up[0]
    arrived = lax.all_to_all(outgoing, "ep", split_axis=1, concat_axis=1, tiled=True)
    fanned = jnp.repeat(arrived, span, axis=0)
    hidden = expert_front(
        lax.all_to_all(fanned, "grp", split_axis=0, concat_axis=0, tiled=True), gate_slice, up_slice
    )
    my_index = lax.axis_index("grp")
    assembled = hidden
    for level in range(span.bit_length() - 1):
        partner = swapped(assembled, "grp", level)
        upper = my_index // (1 << level) % 2
        assembled = jnp.where(
            upper == 0,
            jnp.concatenate([assembled, partner], axis=3),
            jnp.concatenate([partner, assembled], axis=3),
        )
    expert_out = jnp.einsum(
        "abmf,fc->abmc", assembled, w_down[0], preferred_element_type=jnp.float32
    ).astype(jnp.bfloat16)
    returned = lax.all_to_all(expert_out, "grp", split_axis=0, concat_axis=3, tiled=True)
    returned = returned.reshape(n_ep, capacity, 2, width)
    home = lax.all_to_all(returned, "ep", split_axis=0, concat_axis=0, tiled=True)
    back_slot = flat_ids // 2 * (capacity * 2) + ranking * 2 + flat_ids % 2
    matches = back_slot.reshape(tok_rows, top_count)[:, :, None] == slot_ids[None, None, :]
    weight_table = jnp.sum(jnp.where(matches, gate_weights[:, :, None], jnp.float32(0.0)), axis=1)
    combined = jnp.dot(
        weight_table,
        home.reshape(slots, width).astype(jnp.float32),
        precision=lax.Precision.HIGHEST,
    )
    mixed = tokens.astype(jnp.float32) + combined
    factor = lax.rsqrt(jnp.mean(mixed * mixed, axis=1, keepdims=True) + 1e-06)
    return (mixed * factor * norm_gain).astype(jnp.bfloat16)


def shards(tokens, *rest):
    all_rows = tokens.shape[0] * lax.axis_size("grp") * lax.axis_size("ep")
    dense = lax.axis_size("grp") == 4 and lax.axis_size("ep") == 8 and all_rows <= 256
    return (fused if dense else routed)(tokens, *rest)


def solution(mesh):
    placed = (
        P(("grp", "ep"), None),
        P(("grp", "ep"), None),
        P(("grp", "ep"), None),
        P("ep", None, "grp"),
        P("ep", None, "grp"),
        P("ep", None, "grp"),
        P(),
    )
    return jax.shard_map(
        shards, mesh=mesh, in_specs=placed, out_specs=P(("grp", "ep"), None), check_vma=False
    )
```

```python
import functools

import jax
import jax.numpy as jnp
from jax import lax
from jax.experimental import pallas as pl
from jax.experimental.pallas import tpu as pltpu
from jax.sharding import PartitionSpec as P

LANES = 128
MESH = pl.DeviceIdType.MESH


def dot32(a, b):
    return jnp.dot(a, b, preferred_element_type=jnp.float32)


def fused_kernel(
    nz, experts,
    tok_hbm, ids_hbm, gates_hbm, gain_hbm, wg_hbm, wu_hbm, wd_hbm, out_ref,
    tok_ref, ids_ref, gates_ref, gain_ref, wgu, wd, xb, lhs, tabs, hid, part_out, part_in, ret_out, ret_in, near, far_in, fin_out, fin_in,
    t_sem, w_sem, z_sem, x_sem, y_sem, dx_sem, dy_sem, sib_sem, hid_sem, part_sem, ret_sem, far_sem, fin_sem,
):
    f32, bf16 = jnp.float32, jnp.bfloat16
    rows, width = tok_ref.shape
    half = width // 2
    quarter = width // 4
    block = 2 * rows
    stage = 2 * nz * block
    piece = quarter // 2
    ff_part = wgu.shape[2] // 2
    ff_half = 2 * ff_part
    g, p = lax.axis_index("grp"), lax.axis_index("ep")
    y, x = g // 2, g % 2
    z, c = p // 2, p % 2
    ox, oy, oc = 1 - x, 1 - y, 1 - c

    def dev(xx, yy, zz, cc):
        return (yy * 2 + xx, zz * 2 + cc)

    def along(i):
        return (z // 2 * 2 + (z + i) % 2 + i // 2 * 2) % nz

    def remote(src, dst, sems, idx, to):
        return pltpu.make_async_remote_copy(
            src_ref=src, dst_ref=dst, send_sem=sems.at[0, idx], recv_sem=sems.at[1, idx],
            device_id=to, device_id_type=MESH,
        )

    sibling = dev(x, y, z, oc)
    x_peer = dev(ox, y, z, c)
    y_peer = dev(x, oy, z, c)
    x_sibling = dev(ox, y, z, oc)

    small = [
        pltpu.make_async_copy(src, dst, t_sem.at[n])
        for n, (src, dst) in enumerate(
            ((tok_hbm, tok_ref), (ids_hbm, ids_ref), (gates_hbm, gates_ref), (gain_hbm, gain_ref))
        )
    ]
    for load in small:
        load.start()

    loads = []
    for n in range(2):
        for k, src in enumerate((wg_hbm, wu_hbm)):
            from_cols, to_cols = pl.ds(n * ff_part, ff_part), pl.ds(k * ff_part, ff_part)
            loads.append(
                pltpu.make_async_copy(src.at[0, :, from_cols], wgu.at[n, :, to_cols], w_sem.at[len(loads)])
            )
    for mine, at_k in ((0, x), (1, ox)):
        span = pl.ds(pl.multiple_of(at_k * ff_half, ff_half), ff_half)
        for e in range(4):
            loads.append(
                pltpu.make_async_copy(
                    wd_hbm.at[0, span, pl.ds(e * piece, piece)],
                    wd.at[e, pl.ds(mine * ff_half, ff_half), :],
                    w_sem.at[len(loads)],
                )
            )

    barrier = pltpu.get_barrier_semaphore()
    greeted = 0
    for to in [dev(x, (y + dy) % 2, (z + dz) % nz, c) for dy in range(2) for dz in range(nz) if dy or dz] + [
        x_peer, sibling, x_sibling
    ]:
        pl.semaphore_signal(barrier, inc=1, device_id=to, device_id_type=MESH)
        greeted += 1
    for load in small:
        load.wait()
    for load in loads:
        load.start()

    lane = lax.broadcasted_iota(jnp.int32, (rows, LANES), 1)
    table = jnp.zeros((rows, LANES), f32)
    for k in range(ids_ref.shape[1]):
        table += jnp.where(ids_ref[:, k : k + 1] == lane % experts, gates_ref[:, k : k + 1], f32(0.0))
    tok = tok_ref[...].astype(f32)
    high = table.astype(bf16)
    rest = table - high.astype(f32)
    middle = rest.astype(bf16)
    low = (rest - middle.astype(f32)).astype(bf16)
    part = lane // experts
    coded = jnp.where(
        part == 0, high.astype(f32),
        jnp.where(part == 1, middle.astype(f32), jnp.where(part == 2, low.astype(f32), f32(0.0))),
    )

    def spot(xx, i):
        return pl.ds(pl.multiple_of((2 * i + xx) * block, block), block)

    def pair(i):
        return slice(2 * i * block, 2 * (i + 1) * block)

    xb[c, 0, spot(x, 0), :] = jnp.concatenate(
        [
            jnp.concatenate([tok[:, :half], coded], axis=1),
            jnp.concatenate([tok[:, half:], jnp.zeros_like(coded)], axis=1),
        ],
        axis=0,
    ).astype(bf16)

    pl.semaphore_wait(barrier, greeted)
    sends = []

    def go(copy):
        copy.start()
        sends.append(copy)

    z_copy = [None] + [
        remote(xb.at[c, 0, spot(x, 0), :], xb.at[c, 0, spot(x, i), :], z_sem, i, dev(x, y, along(i), c))
        for i in range(1, nz)
    ]
    x_copy = [remote(xb.at[c, 0, spot(x, i), :], xb.at[c, 0, spot(x, i), :], x_sem, i, x_peer) for i in range(nz)]
    x_land = [remote(xb.at[c, 0, spot(ox, i), :], xb.at[c, 0, spot(ox, i), :], x_sem, i, x_peer) for i in range(nz)]
    y_copy = [remote(xb.at[c, 0, spot(x, i), :], xb.at[c, 1, spot(x, i), :], y_sem, i, y_peer) for i in range(nz)]
    by_y = [i for i in range(nz) if i % 4 in (1, 2)]
    d_copy, d_land = [], []
    for i in range(nz):
        if i in by_y:
            d_copy.append(remote(xb.at[c, 0, spot(ox, i), :], xb.at[c, 1, spot(ox, i), :], dy_sem, i, y_peer))
            d_land.append(d_copy[-1])
        else:
            d_copy.append(remote(xb.at[c, 1, spot(x, i), :], xb.at[c, 1, spot(x, i), :], dx_sem, i, x_peer))
            d_land.append(remote(xb.at[c, 1, spot(ox, i), :], xb.at[c, 1, spot(ox, i), :], dx_sem, i, x_peer))
    sib_copy, sib_land = [
        [
            [remote(xb.at[k, s, pair(i), :], xb.at[k, s, pair(i), :], sib_sem, s * nz + i, sibling) for i in range(nz)]
            for s in range(2)
        ]
        for k in (c, oc)
    ]

    def assemble(s, i):
        sib_land[s][i].wait_recv()
        for b in (2 * i, 2 * i + 1):
            at = slice(b * block, (b + 1) * block)
            two = [xb[k, s, at, :].astype(f32) for k in range(2)]
            for h in range(2):
                lhs[s, at, h * half : (h + 1) * half] = jnp.concatenate(
                    [v[h * rows : (h + 1) * rows, :half] for v in two], axis=0
                ).astype(bf16)
            tabs[s, at, :] = jnp.concatenate([v[:rows, half:] for v in two], axis=0)

    for i in range(1, nz):
        go(z_copy[i])
    go(x_copy[0])
    go(y_copy[0])
    def onward(i):
        z_copy[i].wait_recv()
        go(x_copy[i])
        go(y_copy[i])

    def arrive(i):
        x_land[i].wait_recv()
        if i in by_y:
            go(d_copy[i])
        go(sib_copy[0][i])
        y_copy[i].wait_recv()
        if i not in by_y:
            go(d_copy[i])

    def arrive_far(i):
        d_land[i].wait_recv()
        go(sib_copy[1][i])

    chunks = [(0, 0, range(nz)), (1, 1, range(nz))]

    def rows_in(pairs):
        return slice(2 * pairs[0] * block, 2 * (pairs[-1] + 1) * block)

    def hid_copy(chunk, n):
        number, s, pairs = chunk
        at = rows_in(pairs)
        return remote(hid.at[s, n, at], hid.at[s, 2 + n, at], hid_sem, 2 * number + n, x_peer)

    def front(chunk):
        number, s, pairs = chunk
        at = rows_in(pairs)
        assemble(s, pairs[-1])
        if number == 0:
            for load in loads[:4]:
                load.wait()

        @pl.loop(0, 2)
        def _(n):
            both = dot32(lhs[s, at], wgu[n])
            gate, up = both[:, :ff_part], both[:, ff_part:]
            hid[s, n, at] = (gate / (f32(1.0) + jnp.exp(-gate)) * up).astype(bf16)
            hid_copy(chunk, n).start()

    def part_copy(chunk, e):
        number, s, pairs = chunk
        at = rows_in(pairs)
        return remote(part_out.at[s, e, at], part_in.at[s, e, at], part_sem, 2 * number + e, sibling)

    lanes = lax.broadcasted_iota(jnp.int32, (stage, LANES), 1)
    wanted = (lanes % experts == 2 * p + y) & (lanes < 3 * experts)

    def ret_copy(s, e, i):
        to = dev(x, (oy if s else y), along(i), c)
        slot = (s * 2 + e) * nz + i
        return remote(ret_out.at[s, e, pair(i), :], ret_in.at[slot], ret_sem, slot, to)

    def piece_of(chunk, which, e):
        number, s, pairs = chunk
        at = rows_in(pairs)
        total = dot32(jnp.concatenate([hid[s, n, at] for n in range(4)], axis=1), wd[which * 2 + e])
        weight = jnp.sum(jnp.where(wanted, tabs[s, at], f32(0.0)), axis=1, keepdims=True)
        return total * weight

    def back_theirs(chunk):
        number, s, pairs = chunk
        at = rows_in(pairs)
        if number == 0:
            for load in loads[4:]:
                load.wait()
        for n in range(2):
            hid_copy(chunk, n).wait_recv()

        for e in turns(s):
            part_out[s, e, at] = piece_of(chunk, oc, e).astype(bf16)
            part_copy(chunk, e).start()

    def turns(s):
        return (0, 1) if s else (1, 0)

    parts_y = [slice((1 - m) * stage // 2, (2 - m) * stage // 2) for m in range(2)]
    y_sum = [
        remote(ret_out.at[1, 0, at], far_in.at[at], far_sem, m, y_peer) for m, at in enumerate(parts_y)
    ]

    def back_mine(chunk):
        number, s, pairs = chunk
        at = rows_in(pairs)
        for e in turns(s):
            own = piece_of(chunk, c, e)
            part_copy(chunk, e).wait_recv()
            own += part_in[s, e, at].astype(f32)
            if e == 0 and s == 0:
                near[...] = own
                continue
            ret_out[s, e, at] = own.astype(bf16)
            if e == 0:
                for copy in y_sum:
                    go(copy)
                continue
            for i in reversed(pairs):
                if s or i:
                    ret_copy(s, e, i).start()

    def back_near():
        for m, at in enumerate(parts_y):
            y_sum[m].wait_recv()
            ret_out[0, 0, at] = (near[at] + far_in[at].astype(f32)).astype(bf16)
            for i in reversed(range(nz)):
                if i and i // (nz // 2) == 1 - m:
                    ret_copy(0, 0, i).start()

    for i in range(nz):
        if i + 1 < nz:
            onward(i + 1)
        arrive(i)
        if i:
            assemble(0, i - 1)
    front(chunks[0])
    for i in range(nz):
        arrive_far(i)
        if i:
            assemble(1, i - 1)
    front(chunks[1])
    for chunk in chunks:
        back_theirs(chunk)
        back_mine(chunk)
    back_near()

    for e in (1, 0):
        total = ret_out[0, e, pair(0), :].astype(f32)
        for s in range(1 + e):
            for i in range(nz):
                if s or i:
                    ret_copy(s, e, i).wait_recv()
                    total += ret_in[(s * 2 + e) * nz + i].astype(f32)
        fin_out[:, e * piece : (e + 1) * piece] = total

    def rows_of(xx, cc):
        return pl.ds(pl.multiple_of((xx * 2 + cc) * rows, rows), rows)

    fin_copy = [
        remote(fin_out.at[rows_of(xx, cc), :], fin_in.at[n], fin_sem, n, to)
        for n, (xx, cc, to) in enumerate(((ox, c, x_peer), (ox, oc, x_sibling), (x, oc, sibling)))
    ]
    for copy in fin_copy:
        go(copy)
    kept = fin_out[rows_of(x, c), :]
    for copy in fin_copy:
        copy.wait_recv()
    pieces = []
    for h in range(2):
        for q in range(2):
            near = jnp.where(c == q, kept, fin_in[2])
            far = jnp.where(c == q, fin_in[0], fin_in[1])
            pieces.append(jnp.where(x == h, near, far))
    mixed = tok + jnp.concatenate(pieces, axis=1)
    factor = lax.rsqrt(jnp.mean(mixed * mixed, axis=1, keepdims=True) + 1e-06)
    out_ref[...] = (mixed * factor * gain_ref[...]).astype(bf16)
    for chunk in chunks:
        s, pairs = chunk[1:]
        for e in range(2):
            hid_copy(chunk, e).wait_send()
            part_copy(chunk, e).wait_send()
            for i in pairs:
                if (s or i) and (e or not s):
                    ret_copy(s, e, i).wait_send()
    for copy in sends:
        copy.wait_send()


def fused(tokens, expert_ids, gate_weights, w_gate, w_up, w_down, norm_gain):
    f32, bf16 = jnp.float32, jnp.bfloat16
    rows, width = tokens.shape
    n_ep = lax.axis_size("ep")
    nz, experts = n_ep // 2, 2 * n_ep
    half, quarter = width // 2, width // 4
    block = 2 * rows
    stage = 2 * nz * block
    wide = half + LANES
    ff_half = w_gate.shape[2]
    vmem = pltpu.VMEM

    def sems(count):
        return pltpu.SemaphoreType.DMA((2, count))

    return pl.pallas_call(
        functools.partial(fused_kernel, nz, experts),
        out_shape=jax.ShapeDtypeStruct((rows, width), bf16),
        in_specs=[pl.BlockSpec(memory_space=pltpu.HBM)] * 7,
        out_specs=pl.BlockSpec(memory_space=pltpu.VMEM),
        scratch_shapes=[
            vmem((rows, width), bf16),
            vmem(expert_ids.shape, jnp.int32),
            vmem(gate_weights.shape, f32),
            vmem((1, width), f32),
            vmem((2, width, ff_half), bf16),
            vmem((4, 2 * ff_half, quarter // 2), bf16),
            vmem((2, 2, stage, wide), bf16),
            vmem((2, stage, width), bf16),
            vmem((2, stage, LANES), f32),
            vmem((2, 4, stage, ff_half // 2), bf16),
            vmem((2, 2, stage, quarter // 2), bf16),
            vmem((2, 2, stage, quarter // 2), bf16),
            vmem((2, 2, stage, quarter // 2), bf16),
            vmem((4 * nz, 2 * block, quarter // 2), bf16),
            vmem((stage, quarter // 2), f32),
            vmem((stage, quarter // 2), bf16),
            vmem((2 * block, quarter), f32),
            vmem((3, rows, quarter), f32),
            pltpu.SemaphoreType.DMA((4,)),
            pltpu.SemaphoreType.DMA((12,)),
            sems(nz), sems(nz), sems(nz), sems(nz), sems(nz), sems(2 * nz), sems(4), sems(4),
            sems(4 * nz), sems(2), sems(3),
        ],
        compiler_params=pltpu.CompilerParams(
            collective_id=0, has_side_effects=True, vmem_limit_bytes=56 * 1024 * 1024
        ),
    )(tokens, expert_ids, gate_weights, norm_gain.reshape(1, width), w_gate, w_up, w_down)


def swapped(shard, axis, bit):
    return lax.ppermute(shard, axis, [(i, i ^ 1 << bit) for i in range(lax.axis_size(axis))])


def expert_front(arrived, gate_slice, up_slice):
    gate_part = jnp.einsum("abmd,df->abmf", arrived, gate_slice, preferred_element_type=jnp.float32)
    up_part = jnp.einsum("abmd,df->abmf", arrived, up_slice, preferred_element_type=jnp.float32)
    return (jax.nn.silu(gate_part) * up_part).astype(jnp.bfloat16)


def routed(tokens, expert_ids, gate_weights, w_gate, w_up, w_down, norm_gain):
    tok_rows, width = tokens.shape
    top_count = expert_ids.shape[1]
    n_ep = lax.axis_size("ep")
    n_grp = lax.axis_size("grp")
    experts = 2 * n_ep
    capacity = max(2, 2 * tok_rows * top_count // experts)
    slots = experts * capacity
    span = n_grp // 2
    flat_ids = expert_ids.reshape(-1)
    onehot = (flat_ids[:, None] == jnp.arange(experts, dtype=jnp.int32)[None, :]).astype(jnp.int32)
    earlier = jnp.cumsum(onehot, axis=0) - onehot
    ranking = jnp.sum(earlier * onehot, axis=1)
    slot_ids = jnp.arange(slots, dtype=jnp.int32)
    send_slot = flat_ids % 2 * (n_ep * capacity) + flat_ids // 2 * capacity + ranking
    placing = send_slot.reshape(tok_rows, top_count)[None, :, :] == slot_ids[:, None, None]
    placing = jnp.sum(placing.astype(jnp.float32), axis=2).astype(jnp.bfloat16)
    outgoing = jnp.dot(placing, tokens, preferred_element_type=jnp.float32).astype(jnp.bfloat16)
    outgoing = outgoing.reshape(2, n_ep, capacity, width)
    gate_slice = w_gate[0]
    up_slice = w_up[0]
    arrived = lax.all_to_all(outgoing, "ep", split_axis=1, concat_axis=1, tiled=True)
    fanned = jnp.repeat(arrived, span, axis=0)
    hidden = expert_front(
        lax.all_to_all(fanned, "grp", split_axis=0, concat_axis=0, tiled=True), gate_slice, up_slice
    )
    my_index = lax.axis_index("grp")
    assembled = hidden
    for level in range(span.bit_length() - 1):
        partner = swapped(assembled, "grp", level)
        upper = my_index // (1 << level) % 2
        assembled = jnp.where(
            upper == 0,
            jnp.concatenate([assembled, partner], axis=3),
            jnp.concatenate([partner, assembled], axis=3),
        )
    expert_out = jnp.einsum(
        "abmf,fc->abmc", assembled, w_down[0], preferred_element_type=jnp.float32
    ).astype(jnp.bfloat16)
    returned = lax.all_to_all(expert_out, "grp", split_axis=0, concat_axis=3, tiled=True)
    returned = returned.reshape(n_ep, capacity, 2, width)
    home = lax.all_to_all(returned, "ep", split_axis=0, concat_axis=0, tiled=True)
    back_slot = flat_ids // 2 * (capacity * 2) + ranking * 2 + flat_ids % 2
    matches = back_slot.reshape(tok_rows, top_count)[:, :, None] == slot_ids[None, None, :]
    weight_table = jnp.sum(jnp.where(matches, gate_weights[:, :, None], jnp.float32(0.0)), axis=1)
    combined = jnp.dot(
        weight_table,
        home.reshape(slots, width).astype(jnp.float32),
        precision=lax.Precision.HIGHEST,
    )
    mixed = tokens.astype(jnp.float32) + combined
    factor = lax.rsqrt(jnp.mean(mixed * mixed, axis=1, keepdims=True) + 1e-06)
    return (mixed * factor * norm_gain).astype(jnp.bfloat16)


def shards(tokens, *rest):
    all_rows = tokens.shape[0] * lax.axis_size("grp") * lax.axis_size("ep")
    dense = lax.axis_size("grp") == 4 and lax.axis_size("ep") == 8 and all_rows <= 256
    return (fused if dense else routed)(tokens, *rest)


def solution(mesh):
    placed = (
        P(("grp", "ep"), None),
        P(("grp", "ep"), None),
        P(("grp", "ep"), None),
        P("ep", None, "grp"),
        P("ep", None, "grp"),
        P("ep", None, "grp"),
        P(),
    )
    return jax.shard_map(
        shards, mesh=mesh, in_specs=placed, out_specs=P(("grp", "ep"), None), check_vma=False
    )
```

```python
import functools

import jax
import jax.numpy as jnp
from jax import lax
from jax.experimental import pallas as pl
from jax.experimental.pallas import tpu as pltpu
from jax.sharding import PartitionSpec as P

LANES = 128
MESH = pl.DeviceIdType.MESH


def dot32(a, b):
    return jnp.dot(a, b, preferred_element_type=jnp.float32)


def fused_kernel(
    nz, experts,
    tok_hbm, ids_hbm, gates_hbm, gain_hbm, wg_hbm, wu_hbm, wd_hbm, out_ref,
    tok_ref, ids_ref, gates_ref, gain_ref, wgu, wd, xb, lhs, tabs, hid, part_out, part_in, ret_out, ret_in, fin_out, fin_in,
    t_sem, w_sem, z_sem, x_sem, y_sem, dx_sem, dy_sem, sib_sem, hid_sem, part_sem, ret_sem, fin_sem,
):
    f32, bf16 = jnp.float32, jnp.bfloat16
    rows, width = tok_ref.shape
    half = width // 2
    quarter = width // 4
    block = 2 * rows
    stage = 2 * nz * block
    piece = quarter // 2
    ff_part = wgu.shape[2] // 2
    ff_half = 2 * ff_part
    g, p = lax.axis_index("grp"), lax.axis_index("ep")
    y, x = g // 2, g % 2
    z, c = p // 2, p % 2
    ox, oy, oc = 1 - x, 1 - y, 1 - c

    def dev(xx, yy, zz, cc):
        return (yy * 2 + xx, zz * 2 + cc)

    def along(i):
        return (z // 2 * 2 + (z + i) % 2 + i // 2 * 2) % nz

    def remote(src, dst, sems, idx, to):
        return pltpu.make_async_remote_copy(
            src_ref=src, dst_ref=dst, send_sem=sems.at[0, idx], recv_sem=sems.at[1, idx],
            device_id=to, device_id_type=MESH,
        )

    sibling = dev(x, y, z, oc)
    x_peer = dev(ox, y, z, c)
    y_peer = dev(x, oy, z, c)
    x_sibling = dev(ox, y, z, oc)

    small = [
        pltpu.make_async_copy(src, dst, t_sem.at[n])
        for n, (src, dst) in enumerate(
            ((tok_hbm, tok_ref), (ids_hbm, ids_ref), (gates_hbm, gates_ref), (gain_hbm, gain_ref))
        )
    ]
    for load in small:
        load.start()

    loads = []
    for n in range(2):
        for k, src in enumerate((wg_hbm, wu_hbm)):
            from_cols, to_cols = pl.ds(n * ff_part, ff_part), pl.ds(k * ff_part, ff_part)
            loads.append(
                pltpu.make_async_copy(src.at[0, :, from_cols], wgu.at[n, :, to_cols], w_sem.at[len(loads)])
            )
    for mine, at_k in ((0, x), (1, ox)):
        span = pl.ds(pl.multiple_of(at_k * ff_half, ff_half), ff_half)
        for e in range(4):
            loads.append(
                pltpu.make_async_copy(
                    wd_hbm.at[0, span, pl.ds(e * piece, piece)],
                    wd.at[e, pl.ds(mine * ff_half, ff_half), :],
                    w_sem.at[len(loads)],
                )
            )

    barrier = pltpu.get_barrier_semaphore()
    greeted = 0
    for to in [dev(x, (y + dy) % 2, (z + dz) % nz, c) for dy in range(2) for dz in range(nz) if dy or dz] + [
        x_peer, sibling, x_sibling
    ]:
        pl.semaphore_signal(barrier, inc=1, device_id=to, device_id_type=MESH)
        greeted += 1
    for load in small:
        load.wait()

    lane = lax.broadcasted_iota(jnp.int32, (rows, LANES), 1)
    table = jnp.zeros((rows, LANES), f32)
    for k in range(ids_ref.shape[1]):
        table += jnp.where(ids_ref[:, k : k + 1] == lane % experts, gates_ref[:, k : k + 1], f32(0.0))
    tok = tok_ref[...].astype(f32)
    high = table.astype(bf16)
    rest = table - high.astype(f32)
    middle = rest.astype(bf16)
    low = (rest - middle.astype(f32)).astype(bf16)
    part = lane // experts
    coded = jnp.where(
        part == 0, high.astype(f32),
        jnp.where(part == 1, middle.astype(f32), jnp.where(part == 2, low.astype(f32), f32(0.0))),
    )

    def spot(xx, i):
        return pl.ds(pl.multiple_of((2 * i + xx) * block, block), block)

    def pair(i):
        return slice(2 * i * block, 2 * (i + 1) * block)

    xb[c, 0, spot(x, 0), :] = jnp.concatenate(
        [
            jnp.concatenate([tok[:, :half], coded], axis=1),
            jnp.concatenate([tok[:, half:], jnp.zeros_like(coded)], axis=1),
        ],
        axis=0,
    ).astype(bf16)

    pl.semaphore_wait(barrier, greeted)
    sends = []

    def go(copy):
        copy.start()
        sends.append(copy)

    z_copy = [None] + [
        remote(xb.at[c, 0, spot(x, 0), :], xb.at[c, 0, spot(x, i), :], z_sem, i, dev(x, y, along(i), c))
        for i in range(1, nz)
    ]
    x_copy = [remote(xb.at[c, 0, spot(x, i), :], xb.at[c, 0, spot(x, i), :], x_sem, i, x_peer) for i in range(nz)]
    x_land = [remote(xb.at[c, 0, spot(ox, i), :], xb.at[c, 0, spot(ox, i), :], x_sem, i, x_peer) for i in range(nz)]
    y_copy = [remote(xb.at[c, 0, spot(x, i), :], xb.at[c, 1, spot(x, i), :], y_sem, i, y_peer) for i in range(nz)]
    by_y = [i for i in range(nz) if i % 4 in (1, 2)]
    d_copy, d_land = [], []
    for i in range(nz):
        if i in by_y:
            d_copy.append(remote(xb.at[c, 0, spot(ox, i), :], xb.at[c, 1, spot(ox, i), :], dy_sem, i, y_peer))
            d_land.append(d_copy[-1])
        else:
            d_copy.append(remote(xb.at[c, 1, spot(x, i), :], xb.at[c, 1, spot(x, i), :], dx_sem, i, x_peer))
            d_land.append(remote(xb.at[c, 1, spot(ox, i), :], xb.at[c, 1, spot(ox, i), :], dx_sem, i, x_peer))
    sib_copy, sib_land = [
        [
            [remote(xb.at[k, s, pair(i), :], xb.at[k, s, pair(i), :], sib_sem, s * nz + i, sibling) for i in range(nz)]
            for s in range(2)
        ]
        for k in (c, oc)
    ]

    def assemble(s, i):
        sib_land[s][i].wait_recv()
        for b in (2 * i, 2 * i + 1):
            at = slice(b * block, (b + 1) * block)
            two = [xb[k, s, at, :].astype(f32) for k in range(2)]
            for h in range(2):
                lhs[s, at, h * half : (h + 1) * half] = jnp.concatenate(
                    [v[h * rows : (h + 1) * rows, :half] for v in two], axis=0
                ).astype(bf16)
            tabs[s, at, :] = jnp.concatenate([v[:rows, half:] for v in two], axis=0)

    for i in range(1, nz):
        go(z_copy[i])
    go(x_copy[0])
    go(y_copy[0])
    for load in loads:
        load.start()
    def onward(i):
        z_copy[i].wait_recv()
        go(x_copy[i])
        go(y_copy[i])

    def arrive(i):
        x_land[i].wait_recv()
        if i in by_y:
            go(d_copy[i])
        go(sib_copy[0][i])
        y_copy[i].wait_recv()
        if i not in by_y:
            go(d_copy[i])

    def arrive_far(i):
        d_land[i].wait_recv()
        go(sib_copy[1][i])

    chunks = [(0, 0, range(nz)), (1, 1, range(nz))]

    def rows_in(pairs):
        return slice(2 * pairs[0] * block, 2 * (pairs[-1] + 1) * block)

    def hid_copy(chunk, n):
        number, s, pairs = chunk
        at = rows_in(pairs)
        return remote(hid.at[s, n, at], hid.at[s, 2 + n, at], hid_sem, 2 * number + n, x_peer)

    def front(chunk, n):
        number, s, pairs = chunk
        at = rows_in(pairs)
        both = dot32(lhs[s, at], wgu[n])
        gate, up = both[:, :ff_part], both[:, ff_part:]
        hid[s, n, at] = (gate / (f32(1.0) + jnp.exp(-gate)) * up).astype(bf16)
        hid_copy(chunk, n).start()

    def part_copy(chunk, e):
        number, s, pairs = chunk
        at = rows_in(pairs)
        return remote(part_out.at[s, e, at], part_in.at[s, e, at], part_sem, 2 * number + e, sibling)

    lanes = lax.broadcasted_iota(jnp.int32, (stage, LANES), 1)
    wanted = (lanes % experts == 2 * p + y) & (lanes < 3 * experts)

    def ret_copy(s, e, i):
        to = dev(x, (oy if s else y), along(i), c)
        slot = (s * 2 + e) * nz + i
        return remote(ret_out.at[s, e, pair(i), :], ret_in.at[slot], ret_sem, slot, to)

    def piece_of(chunk, which, e):
        number, s, pairs = chunk
        at = rows_in(pairs)
        total = dot32(jnp.concatenate([hid[s, n, at] for n in range(4)], axis=1), wd[which * 2 + e])
        weight = jnp.sum(jnp.where(wanted, tabs[s, at], f32(0.0)), axis=1, keepdims=True)
        return total * weight

    def back_theirs(chunk):
        number, s, pairs = chunk
        at = rows_in(pairs)
        if number == 0:
            for load in loads[4:]:
                load.wait()
        for n in range(2):
            hid_copy(chunk, n).wait_recv()

        @pl.loop(0, 2)
        def _(e):
            part_out[s, e, at] = piece_of(chunk, oc, e).astype(bf16)
            part_copy(chunk, e).start()

    def back_mine(chunk):
        number, s, pairs = chunk
        at = rows_in(pairs)

        @pl.loop(0, 2)
        def _(e):
            own = piece_of(chunk, c, e)
            part_copy(chunk, e).wait_recv()
            ret_out[s, e, at] = (own + part_in[s, e, at].astype(f32)).astype(bf16)
            for i in reversed(pairs):
                if s or i:
                    ret_copy(s, e, i).start()

    for i in range(nz):
        if i + 1 < nz:
            onward(i + 1)
        arrive(i)
        if i:
            assemble(0, i - 1)
    assemble(0, nz - 1)
    for load in loads[:4]:
        load.wait()
    front(chunks[0], 0)
    for i in range(nz):
        arrive_far(i)
    front(chunks[0], 1)
    for i in range(nz):
        assemble(1, i)
    for n in range(2):
        front(chunks[1], n)
    for chunk in chunks:
        back_theirs(chunk)
        back_mine(chunk)

    for e in range(2):
        total = ret_out[0, e, pair(0), :].astype(f32)
        for s in range(2):
            for i in range(nz):
                if s or i:
                    ret_copy(s, e, i).wait_recv()
                    total += ret_in[(s * 2 + e) * nz + i].astype(f32)
        fin_out[:, e * piece : (e + 1) * piece] = total

    def rows_of(xx, cc):
        return pl.ds(pl.multiple_of((xx * 2 + cc) * rows, rows), rows)

    fin_copy = [
        remote(fin_out.at[rows_of(xx, cc), :], fin_in.at[n], fin_sem, n, to)
        for n, (xx, cc, to) in enumerate(((ox, c, x_peer), (ox, oc, x_sibling), (x, oc, sibling)))
    ]
    for copy in fin_copy:
        go(copy)
    kept = fin_out[rows_of(x, c), :]
    for copy in fin_copy:
        copy.wait_recv()
    pieces = []
    for h in range(2):
        for q in range(2):
            near = jnp.where(c == q, kept, fin_in[2])
            far = jnp.where(c == q, fin_in[0], fin_in[1])
            pieces.append(jnp.where(x == h, near, far))
    mixed = tok + jnp.concatenate(pieces, axis=1)
    factor = lax.rsqrt(jnp.mean(mixed * mixed, axis=1, keepdims=True) + 1e-06)
    out_ref[...] = (mixed * factor * gain_ref[...]).astype(bf16)
    for chunk in chunks:
        s, pairs = chunk[1:]
        for e in range(2):
            hid_copy(chunk, e).wait_send()
            part_copy(chunk, e).wait_send()
            for i in pairs:
                if s or i:
                    ret_copy(s, e, i).wait_send()
    for copy in sends:
        copy.wait_send()


def fused(tokens, expert_ids, gate_weights, w_gate, w_up, w_down, norm_gain):
    f32, bf16 = jnp.float32, jnp.bfloat16
    rows, width = tokens.shape
    n_ep = lax.axis_size("ep")
    nz, experts = n_ep // 2, 2 * n_ep
    half, quarter = width // 2, width // 4
    block = 2 * rows
    stage = 2 * nz * block
    wide = half + LANES
    ff_half = w_gate.shape[2]
    vmem = pltpu.VMEM

    def sems(count):
        return pltpu.SemaphoreType.DMA((2, count))

    return pl.pallas_call(
        functools.partial(fused_kernel, nz, experts),
        out_shape=jax.ShapeDtypeStruct((rows, width), bf16),
        in_specs=[pl.BlockSpec(memory_space=pltpu.HBM)] * 7,
        out_specs=pl.BlockSpec(memory_space=pltpu.VMEM),
        scratch_shapes=[
            vmem((rows, width), bf16),
            vmem(expert_ids.shape, jnp.int32),
            vmem(gate_weights.shape, f32),
            vmem((1, width), f32),
            vmem((2, width, ff_half), bf16),
            vmem((4, 2 * ff_half, quarter // 2), bf16),
            vmem((2, 2, stage, wide), bf16),
            vmem((2, stage, width), bf16),
            vmem((2, stage, LANES), f32),
            vmem((2, 4, stage, ff_half // 2), bf16),
            vmem((2, 2, stage, quarter // 2), bf16),
            vmem((2, 2, stage, quarter // 2), bf16),
            vmem((2, 2, stage, quarter // 2), bf16),
            vmem((4 * nz, 2 * block, quarter // 2), bf16),
            vmem((2 * block, quarter), f32),
            vmem((3, rows, quarter), f32),
            pltpu.SemaphoreType.DMA((4,)),
            pltpu.SemaphoreType.DMA((12,)),
            sems(nz), sems(nz), sems(nz), sems(nz), sems(nz), sems(2 * nz), sems(4), sems(4),
            sems(4 * nz), sems(3),
        ],
        compiler_params=pltpu.CompilerParams(
            collective_id=0, has_side_effects=True, vmem_limit_bytes=56 * 1024 * 1024
        ),
    )(tokens, expert_ids, gate_weights, norm_gain.reshape(1, width), w_gate, w_up, w_down)


def swapped(shard, axis, bit):
    return lax.ppermute(shard, axis, [(i, i ^ 1 << bit) for i in range(lax.axis_size(axis))])


def expert_front(arrived, gate_slice, up_slice):
    gate_part = jnp.einsum("abmd,df->abmf", arrived, gate_slice, preferred_element_type=jnp.float32)
    up_part = jnp.einsum("abmd,df->abmf", arrived, up_slice, preferred_element_type=jnp.float32)
    return (jax.nn.silu(gate_part) * up_part).astype(jnp.bfloat16)


def routed(tokens, expert_ids, gate_weights, w_gate, w_up, w_down, norm_gain):
    tok_rows, width = tokens.shape
    top_count = expert_ids.shape[1]
    n_ep = lax.axis_size("ep")
    n_grp = lax.axis_size("grp")
    experts = 2 * n_ep
    capacity = max(2, 2 * tok_rows * top_count // experts)
    slots = experts * capacity
    span = n_grp // 2
    flat_ids = expert_ids.reshape(-1)
    onehot = (flat_ids[:, None] == jnp.arange(experts, dtype=jnp.int32)[None, :]).astype(jnp.int32)
    earlier = jnp.cumsum(onehot, axis=0) - onehot
    ranking = jnp.sum(earlier * onehot, axis=1)
    slot_ids = jnp.arange(slots, dtype=jnp.int32)
    send_slot = flat_ids % 2 * (n_ep * capacity) + flat_ids // 2 * capacity + ranking
    placing = send_slot.reshape(tok_rows, top_count)[None, :, :] == slot_ids[:, None, None]
    placing = jnp.sum(placing.astype(jnp.float32), axis=2).astype(jnp.bfloat16)
    outgoing = jnp.dot(placing, tokens, preferred_element_type=jnp.float32).astype(jnp.bfloat16)
    outgoing = outgoing.reshape(2, n_ep, capacity, width)
    gate_slice = w_gate[0]
    up_slice = w_up[0]
    arrived = lax.all_to_all(outgoing, "ep", split_axis=1, concat_axis=1, tiled=True)
    fanned = jnp.repeat(arrived, span, axis=0)
    hidden = expert_front(
        lax.all_to_all(fanned, "grp", split_axis=0, concat_axis=0, tiled=True), gate_slice, up_slice
    )
    my_index = lax.axis_index("grp")
    assembled = hidden
    for level in range(span.bit_length() - 1):
        partner = swapped(assembled, "grp", level)
        upper = my_index // (1 << level) % 2
        assembled = jnp.where(
            upper == 0,
            jnp.concatenate([assembled, partner], axis=3),
            jnp.concatenate([partner, assembled], axis=3),
        )
    expert_out = jnp.einsum(
        "abmf,fc->abmc", assembled, w_down[0], preferred_element_type=jnp.float32
    ).astype(jnp.bfloat16)
    returned = lax.all_to_all(expert_out, "grp", split_axis=0, concat_axis=3, tiled=True)
    returned = returned.reshape(n_ep, capacity, 2, width)
    home = lax.all_to_all(returned, "ep", split_axis=0, concat_axis=0, tiled=True)
    back_slot = flat_ids // 2 * (capacity * 2) + ranking * 2 + flat_ids % 2
    matches = back_slot.reshape(tok_rows, top_count)[:, :, None] == slot_ids[None, None, :]
    weight_table = jnp.sum(jnp.where(matches, gate_weights[:, :, None], jnp.float32(0.0)), axis=1)
    combined = jnp.dot(
        weight_table,
        home.reshape(slots, width).astype(jnp.float32),
        precision=lax.Precision.HIGHEST,
    )
    mixed = tokens.astype(jnp.float32) + combined
    factor = lax.rsqrt(jnp.mean(mixed * mixed, axis=1, keepdims=True) + 1e-06)
    return (mixed * factor * norm_gain).astype(jnp.bfloat16)


def shards(tokens, *rest):
    all_rows = tokens.shape[0] * lax.axis_size("grp") * lax.axis_size("ep")
    dense = lax.axis_size("grp") == 4 and lax.axis_size("ep") == 8 and all_rows <= 256
    return (fused if dense else routed)(tokens, *rest)


def solution(mesh):
    placed = (
        P(("grp", "ep"), None),
        P(("grp", "ep"), None),
        P(("grp", "ep"), None),
        P("ep", None, "grp"),
        P("ep", None, "grp"),
        P("ep", None, "grp"),
        P(),
    )
    return jax.shard_map(
        shards, mesh=mesh, in_specs=placed, out_specs=P(("grp", "ep"), None), check_vma=False
    )
```
